32 devices in a mesh: seq: 8 (over z, core), mp: 2 (over y), dp: 2 (over x).
Axes of the slice: x: 2, y: 2, z: 4, core: 2. Of those that a mesh axis runs over, the one named last changes fastest.
Arguments:
- latents: bfloat16 [2, 1536, 1792], P('dp', 'seq', 'mp'), may hold values from -6 to 6
- grad_out: bfloat16 [2, 1536, 1792], P('dp', 'seq', 'mp'), may hold values from -6 to 6
- sync_mod: bfloat16 [2, 1200, 3584], P('dp', 'seq'), may hold values from -3 to 3
- w_qkv: bfloat16 [1792, 3, 1024], P(None, None, 'mp'), may hold values from -0.125 to 0.125
- w_out: bfloat16 [1024, 1792], P('mp'), may hold values from -0.1875 to 0.1875
- q_gain: float32 [8, 128], P('mp'), may hold values from 0.5 to 2.5
- k_gain: float32 [8, 128], P('mp'), may hold values from 0.5 to 2.5
- frame_of: int32 [2, 1536], P('dp', 'seq'), may hold values from 0 to 1199, as said below
- group_id: int32 [2, 1536], P('dp'), may hold values from 0 to 31, never falling along the last dimension, each value on 1 to 96 neighbouring positions
- clip_len: int32 [2], P('dp'), may hold values from 768 to 1536
Outputs:
- mixed: bfloat16 [2, 1536, 1792], P('dp', 'seq', 'mp')
- grad_latents: bfloat16 [2, 1536, 1792], P('dp', 'seq', 'mp')
- grad_wqkv: float32 [1792, 3, 1024], P(('seq', 'dp'), None, 'mp')
- grad_wout: float32 [1024, 1792], P('mp', ('seq', 'dp'))
The draws below stay inside these ranges and needn't reach their ends.
Inputs may be any that keep to these rules, and one draw needn't show every extreme that they name: frame_of[c, l] = floor((96 l + s) / 125) with a phase s of 0 to 124 drawn for each clip, so the latents on seq index j read frames held by seq indices j - 1 and j only.
All inputs are finite; a program needn't handle non-finite values.
Results may differ from the reference program's by a relative error of at most 0.012.
The reference program's roundings to bfloat16 on the way (of `hidden`, `query_norm`, `heads_out`, `grad_heads`, `grad_logits` and `grad_proj`) count: a program that leaves them out, or rounds other values in their place, can miss the bound.
Values may be sent and summed in bfloat16 or wider, within the bound.
No kernel may reach another device: no remote copies, remote signals or barrier semaphores. Data moves between devices by JAX's collectives and lax.ppermute only.
A program may use at most 128 MiB of HBM per device.

```python
import math
import jax
import jax.numpy as jnp
import numpy as np
from jax import lax

D = 1792
HEADS = 8
HD = 128
GROUP = 96
CLIPS = 2
LATENTS = 1536
FRAMES = 1200
GROUPS = 32


def draw_q_gain(key, part):
    sub_key = jax.random.fold_in(key, 11)
    return jax.random.uniform(sub_key, (HEADS, HD), jnp.float32, 0.5, 1.6)


def draw_k_gain(key, part):
    sub_key = jax.random.fold_in(key, 12)
    return jax.random.uniform(sub_key, (HEADS, HD), jnp.float32, 0.5, 1.6)


def draw_frame_of(key, part):
    phases = jax.random.randint(jax.random.fold_in(key, 21), (CLIPS, 1), 0, 125, dtype=jnp.int32)
    positions = lax.iota(jnp.int32, LATENTS)[None, :]
    return ((96 * positions + phases) // 125).astype(jnp.int32)


def steps_of(rng, extent, pieces, least, largest):
    def one(axis_at, shards_of):
        steps = jax.random.uniform(jax.random.fold_in(jax.random.fold_in(rng, 6), axis_at), (shards_of,), jnp.float32, least / len(pieces), largest / len(pieces))
        return jnp.repeat(jnp.exp(steps), extent[axis_at] // shards_of).reshape((-1,) + (1,) * (len(extent) - axis_at - 1))

    level = one(*pieces[0])
    for cut in pieces[1:]:
        level = level * one(*cut)
    return level


def split_up(amount, total, reach, skew):
    loads = [(1 << 20) // math.isqrt(rank ** skew) + 1 for rank in range(2, amount + 1)]
    spare, holding = total - reach - (amount - 1), [1] * (amount - 1)
    while spare > 0:
        free = [i for i in range(amount - 1) if holding[i] < reach]
        pool, budget = sum([loads[i] for i in free]), spare
        for i in free:
            addition = min(reach - holding[i], max(1, budget * loads[i] // pool), spare)
            holding[i] = holding[i] + addition
            spare = spare - addition
    return np.array([reach] + holding)


def ragged(rng, number_of, total, reach, skew):
    if number_of == 2:
        one = jax.random.randint(rng, (), max(1, total - reach), min(reach, total - 1) + 1)
        return jnp.stack([one, total - one])
    tallies = jnp.asarray(split_up(number_of, total, reach, skew), jnp.int32)
    couples = (number_of - 1) // 2
    giver, taker = tallies[1:1 + 2 * couples:2], tallies[2:2 + 2 * couples:2]
    room = jnp.minimum(giver - 1, reach - taker)
    passed = jax.random.randint(jax.random.fold_in(rng, 1), (couples,), 0, 1 << 20) % (room + 1)
    tallies = tallies.at[1:1 + 2 * couples:2].set(giver - passed).at[2:2 + 2 * couples:2].set(taker + passed)
    return tallies[jax.random.permutation(jax.random.fold_in(rng, 2), number_of)]


def centred(rng, dims, scale, reach, cuts=(), kind=jnp.bfloat16):
    level = steps_of(rng, dims, cuts, -0.22, 0.18) if cuts else 1.0
    entries = jax.random.normal(rng, dims, jnp.float32) * scale * level
    return jnp.minimum(jnp.maximum(entries, -reach), reach).astype(kind)


def setup_inputs(seed: int = 0) -> dict:
    keys = jax.random.split(jax.random.key(seed), 11)
    latents = centred(keys[0], (CLIPS, LATENTS, D), 1.0, 6.0, ((0, 2), (1, 8), (2, 2)))
    grad_out = centred(keys[1], (CLIPS, LATENTS, D), 1.0, 6.0, ((0, 2), (1, 8), (2, 2)))
    sync_mod = centred(keys[2], (CLIPS, FRAMES, 2 * D), 0.5, 3.0, ((0, 2), (1, 8)))
    w_qkv = centred(keys[3], (D, 3, HEADS * HD), D ** -0.5, 0.125, ((2, 2),))
    w_out = centred(keys[4], (HEADS * HD, D), (HEADS * HD) ** -0.5, 0.1875, ((0, 2),))
    q_gain = draw_q_gain(jax.random.fold_in(keys[10], 71), 0)
    k_gain = draw_k_gain(jax.random.fold_in(keys[10], 71), 0)
    frame_of = draw_frame_of(jax.random.fold_in(keys[10], 71), 0)
    group_id = jax.vmap(lambda own: jnp.searchsorted(jnp.cumsum(ragged(own, GROUPS, LATENTS, GROUP, 1)), jnp.arange(LATENTS), side="right"))(jax.random.split(keys[8], CLIPS)).reshape((CLIPS, LATENTS)).astype(jnp.int32)
    clip_len = jax.random.randint(keys[9], (CLIPS,), LATENTS // 2, LATENTS + 1).astype(jnp.int32)
    return dict(latents=latents, grad_out=grad_out, sync_mod=sync_mod, w_qkv=w_qkv, w_out=w_out, q_gain=q_gain, k_gain=k_gain, frame_of=frame_of, group_id=group_id, clip_len=clip_len)


EPSILON = 1e-06
NEG_FILL = -1e+30

def inv_rms(values):
    return lax.rsqrt(lax.optimization_barrier(jnp.mean(values * values, axis=-1, keepdims=True)) + EPSILON)

def rounded(values):
    return lax.optimization_barrier(values.astype(jnp.bfloat16)).astype(jnp.float32)

def norm_back(raw, inv_norm, gains, upstream):
    inner_dot = lax.optimization_barrier(jnp.mean(upstream * gains * raw, axis=-1, keepdims=True))
    return inv_norm * (gains * upstream - raw * inv_norm * inv_norm * inner_dot)

def clip_attention(operands):
    query_norm, key_norm, values, grad_heads, group_ids, clip_length = operands
    seq_length = query_norm.shape[0]
    factor = query_norm.shape[-1] ** (-0.5)
    positions = lax.iota(jnp.int32, seq_length)
    allowed = ((group_ids[None, :] <= group_ids[:, None]) & (positions[None, :] < clip_length))[None]
    query_f = query_norm.astype(jnp.float32)
    key_f = key_norm.astype(jnp.float32)
    value_f = values.astype(jnp.float32)
    logits = jnp.einsum('qhd,khd->hqk', query_f, key_f) * factor
    logits = jnp.where(allowed, logits, NEG_FILL)
    row_max = lax.optimization_barrier(jnp.max(logits, axis=-1, keepdims=True))
    unnorm = jnp.where(allowed, jnp.exp(logits - row_max), 0.0)
    row_sum = lax.optimization_barrier(jnp.sum(unnorm, axis=-1, keepdims=True))
    heads_out = jnp.einsum('hqk,khd->qhd', rounded(unnorm), value_f) / jnp.transpose(row_sum, (1, 0, 2))
    heads_out = heads_out.astype(jnp.bfloat16)
    upstream = grad_heads.astype(jnp.float32)
    out_dot = lax.optimization_barrier(jnp.sum(upstream * heads_out.astype(jnp.float32), axis=-1))
    probs = unnorm / row_sum
    grad_probs = jnp.einsum('qhd,khd->hqk', upstream, value_f)
    grad_logits = rounded(probs * (grad_probs - jnp.transpose(out_dot)[:, :, None]))
    grad_query = jnp.einsum('hqk,khd->qhd', grad_logits, key_f) * factor
    grad_key = jnp.einsum('hqk,qhd->khd', grad_logits, query_f) * factor
    grad_value = jnp.einsum('hqk,qhd->khd', rounded(probs), upstream)
    return (heads_out, grad_query, grad_key, grad_value)

def reference(latents, grad_out, sync_mod, w_qkv, w_out, q_gain, k_gain, frame_of, group_id, clip_len):
    clip_count, seq_length, model_width = latents.shape
    heads_all, head_dim = q_gain.shape
    inner_width = heads_all * head_dim
    inputs_f = latents.astype(jnp.float32)
    inv_norm = inv_rms(inputs_f)
    normed = inputs_f * inv_norm
    modulation = jax.vmap(lambda lookup_table, row_index: lookup_table[row_index])(sync_mod, frame_of).astype(jnp.float32)
    mod_scale = modulation[:, :, :model_width]
    mod_gate = modulation[:, :, model_width:]
    hidden = (normed * (1.0 + mod_scale)).astype(jnp.bfloat16)
    flat_hidden = hidden.reshape(clip_count * seq_length, model_width)
    flat_weight = w_qkv.reshape(model_width, 3 * inner_width)
    projected = jnp.dot(flat_hidden, flat_weight, preferred_element_type=jnp.float32)
    projected = projected.reshape(clip_count, seq_length, 3, heads_all, head_dim)
    query_raw = projected[:, :, 0]
    key_raw = projected[:, :, 1]
    query_inv = inv_rms(query_raw)
    key_inv = inv_rms(key_raw)
    query_norm = (query_raw * query_inv * q_gain).astype(jnp.bfloat16)
    key_norm = (key_raw * key_inv * k_gain).astype(jnp.bfloat16)
    values = projected[:, :, 2].astype(jnp.bfloat16)
    grad_attn = (grad_out.astype(jnp.float32) * mod_gate).astype(jnp.bfloat16)
    flat_grad = grad_attn.reshape(clip_count * seq_length, model_width)
    grad_heads = jnp.dot(flat_grad, w_out.T, preferred_element_type=jnp.float32).astype(jnp.bfloat16)
    grad_heads = grad_heads.reshape(clip_count, seq_length, heads_all, head_dim)
    heads_out, grad_qnorm, grad_knorm, grad_values = lax.map(clip_attention, (query_norm, key_norm, values, grad_heads, group_id, clip_len))
    out_rows = heads_out.reshape(clip_count * seq_length, inner_width)
    attn = jnp.dot(out_rows, w_out, preferred_element_type=jnp.float32).reshape(clip_count, seq_length, model_width)
    mixed = (inputs_f + mod_gate * attn).astype(jnp.bfloat16)
    grad_wout = jnp.dot(out_rows.T, flat_grad, preferred_element_type=jnp.float32)
    grad_query = norm_back(query_raw, query_inv, q_gain, grad_qnorm)
    grad_key = norm_back(key_raw, key_inv, k_gain, grad_knorm)
    grad_proj = jnp.stack([grad_query, grad_key, grad_values], axis=2).astype(jnp.bfloat16)
    grad_proj = grad_proj.reshape(clip_count * seq_length, 3 * inner_width)
    grad_wqkv = jnp.dot(flat_hidden.T, grad_proj, preferred_element_type=jnp.float32).reshape(model_width, 3, inner_width)
    grad_hidden = jnp.dot(grad_proj, flat_weight.T, preferred_element_type=jnp.float32).reshape(clip_count, seq_length, model_width)
    grad_normed = grad_hidden * (1.0 + mod_scale)
    grad_inputs = inv_norm * (grad_normed - normed * lax.optimization_barrier(jnp.mean(grad_normed * normed, axis=-1, keepdims=True)))
    grad_latents = (grad_out.astype(jnp.float32) + grad_inputs).astype(jnp.bfloat16)
    return (mixed, grad_latents, grad_wqkv, grad_wout)
```

```python
import functools
import math

import jax
import jax.numpy as jnp
from jax import lax
from jax.experimental import pallas as pl
from jax.experimental.pallas import tpu as pltpu
from jax.sharding import PartitionSpec as P

EPSILON = 1e-06
NEG_FILL = -1e30
GROUP_MOST = 96
FRAME_UP, FRAME_DOWN = 96, 125
NO_GROUP = 1 << 30
BF = jnp.bfloat16
F32 = jnp.float32


def swap(value, axis, distance):
    count = lax.axis_size(axis)
    return lax.ppermute(value, axis, [(i, i ^ distance) for i in range(count)])


def unxor(pieces, place):
    pieces = list(pieces)
    for bit in range((len(pieces) - 1).bit_length()):
        odd = ((place >> bit) & 1) == 1
        pieces = [jnp.where(odd, pieces[j ^ (1 << bit)], pieces[j]) for j in range(len(pieces))]
    return pieces


def full_width(value):
    count = lax.axis_size("mp")
    pieces = [value] + [swap(value, "mp", t) for t in range(1, count)]
    return jnp.concatenate(unxor(pieces, lax.axis_index("mp")), axis=-1)


def width_sum(partial, width_part):
    place = lax.axis_index("mp")
    total = lax.dynamic_slice_in_dim(partial, place * width_part, width_part, 1)
    for t in range(1, lax.axis_size("mp")):
        other = lax.dynamic_slice_in_dim(partial, (place ^ t) * width_part, width_part, 1)
        total = total + swap(other.astype(BF), "mp", t).astype(F32)
    return total


def inv_rms(values):
    return lax.rsqrt(jnp.mean(values * values, axis=-1, keepdims=True) + EPSILON)


def norm_back(raw, inv_norm, gains, upstream):
    inner_dot = jnp.mean(upstream * gains * raw, axis=-1, keepdims=True)
    return inv_norm * (gains * upstream - raw * inv_norm * inv_norm * inner_dot)


def round_up(value, step):
    return -(-value // step) * step


def attention_kernel(heads, sharers, rows, block, factor, *refs):
    place_ref, key_group_ref, query_group_ref = refs[:3]
    at = 3
    own = refs[at : at + heads]
    at += heads
    shared = refs[at : at + heads * (sharers - 1)]
    at += heads * (sharers - 1)
    ups = refs[at : at + heads]
    at += heads
    outs = refs[at : at + heads]
    at += heads
    key_grads = refs[at : at + heads * sharers]
    at += heads * sharers
    key_s, value_s, query_s, up_s, out_s, dq_s, dk_s, dv_s = refs[at:]
    head = place_ref[0]
    part = place_ref[1]
    span = heads * sharers * rows
    total = heads * rows
    for t in range(heads):
        m = head ^ t
        query_s[m] = own[t][0]
        up_s[m] = ups[t][...]
        key_s[m * sharers + part] = own[t][1]
        value_s[m * sharers + part] = own[t][2]
        for u in range(1, sharers):
            piece = shared[t * (sharers - 1) + u - 1]
            key_s[m * sharers + (part ^ u)] = piece[0]
            value_s[m * sharers + (part ^ u)] = piece[1]
    dk_s[...] = jnp.zeros_like(dk_s)
    dv_s[...] = jnp.zeros_like(dv_s)
    keys = key_s[...].reshape(span, key_s.shape[-1])
    values = value_s[...].reshape(span, key_s.shape[-1])
    queries = query_s[...].reshape(total, key_s.shape[-1])
    upstream = up_s[...].reshape(total, key_s.shape[-1])
    group_col = jnp.transpose(jnp.broadcast_to(key_group_ref[...], (128, span)))
    group_col = jnp.concatenate([group_col] * (-(-block // 128)), axis=1)[:, :block]
    scale = factor * math.log2(math.e)
    over_last = (((1,), (1,)), ((), ()))
    over_first = (((0,), (0,)), ((), ()))
    for j in range(total // block):
        last = ((j + 1) * block - 1) // rows
        reach = min(span, round_up((last + 1) * sharers * rows + GROUP_MOST - 1, 128))
        lanes = slice(j * block, (j + 1) * block)
        query = queries[lanes]
        up = upstream[lanes]
        key = keys[:reach]
        value = values[:reach]
        logits = lax.dot_general(key, query, over_last, preferred_element_type=F32)
        logits = jnp.where(group_col[:reach] <= query_group_ref[:, lanes], logits, NEG_FILL)
        row_max = jnp.max(logits, axis=0, keepdims=True)
        unnorm = jnp.exp2((logits - row_max) * scale)
        inverse = 1.0 / jnp.sum(unnorm, axis=0, keepdims=True)
        out = lax.dot_general(value, unnorm.astype(BF), over_first, preferred_element_type=F32)
        out = (out * inverse).astype(BF)
        up_t = jnp.transpose(up.astype(F32))
        out_dot = jnp.sum(up_t * out.astype(F32), axis=0, keepdims=True)
        probs = unnorm * inverse
        grad_probs = lax.dot_general(value, up, over_last, preferred_element_type=F32)
        grad_logits = (probs * (grad_probs - out_dot)).astype(BF)
        grad_query = lax.dot_general(key, grad_logits, over_first, preferred_element_type=F32)
        out_s[lanes, :] = jnp.transpose(out.astype(F32)).astype(BF)
        dq_s[lanes, :] = jnp.transpose(grad_query * factor).astype(BF)
        dk_s[:reach, :] += jnp.dot(grad_logits, query, preferred_element_type=F32)
        dv_s[:reach, :] += jnp.dot(probs.astype(BF), up, preferred_element_type=F32)
    for t in range(heads):
        m = head ^ t
        here = pl.ds(pl.multiple_of(m * rows, 64), rows)
        outs[t][0] = out_s[here, :]
        outs[t][1] = dq_s[here, :]
        for u in range(sharers):
            there = pl.ds(pl.multiple_of((m * sharers + (part ^ u)) * rows, 64), rows)
            ref = key_grads[t * sharers + u]
            ref[0] = (dk_s[there, :] * factor).astype(ref.dtype)
            ref[1] = dv_s[there, :].astype(ref.dtype)


def attention(head, part, group_ids, clip_length, own, shared, ups):
    heads = len(own)
    sharers = len(shared) // heads + 1
    rows, width = ups[0].shape
    span = heads * sharers * rows
    total = heads * rows
    block = 256 if total % 256 == 0 else total
    positions = lax.iota(jnp.int32, span)
    key_group = jnp.where(positions < clip_length, group_ids, NO_GROUP)[None, :]
    query_group = lax.dynamic_index_in_dim(
        group_ids.reshape(heads, sharers, rows), part, 1, keepdims=False
    ).reshape(1, total)
    place = jnp.stack([head, part]).astype(jnp.int32)
    vmem = pl.BlockSpec(memory_space=pltpu.VMEM)
    pair = (2, rows, width)
    out_shape = [jax.ShapeDtypeStruct(pair, BF)] * heads
    for _ in range(heads):
        out_shape.append(jax.ShapeDtypeStruct(pair, F32))
        out_shape.extend([jax.ShapeDtypeStruct(pair, BF)] * (sharers - 1))
    got = pl.pallas_call(
        functools.partial(attention_kernel, heads, sharers, rows, block, width ** (-0.5)),
        out_shape=out_shape,
        in_specs=[pl.BlockSpec(memory_space=pltpu.SMEM)]
        + [vmem] * (2 + 2 * heads + heads * (sharers - 1)),
        out_specs=[vmem] * len(out_shape),
        scratch_shapes=[
            pltpu.VMEM((heads * sharers, rows, width), BF),
            pltpu.VMEM((heads * sharers, rows, width), BF),
            pltpu.VMEM((heads, rows, width), BF),
            pltpu.VMEM((heads, rows, width), BF),
            pltpu.VMEM((total, width), BF),
            pltpu.VMEM((total, width), BF),
            pltpu.VMEM((span, width), F32),
            pltpu.VMEM((span, width), F32),
        ],
        compiler_params=pltpu.CompilerParams(vmem_limit_bytes=48 * 1024 * 1024),
        cost_estimate=pl.CostEstimate(
            flops=12 * total * span * width, bytes_accessed=4 << 20, transcendentals=total * span
        ),
        name="attention",
    )(place, key_group, query_group, *own, *shared, *ups)
    outs = got[:heads]
    key_grads = [got[heads + t * sharers : heads + (t + 1) * sharers] for t in range(heads)]
    return outs, key_grads


def weight_grad(left_t, right):
    count, clips = lax.axis_size("seq"), lax.axis_size("dp")
    seq, clip = lax.axis_index("seq"), lax.axis_index("dp")
    core = seq % 2
    span = left_t.shape[0] // (count * clips)
    rows = left_t.shape[1]
    blocks = left_t.reshape(count // 2, 2 * clips, span, rows)
    lefts, rights = [], []
    for w in range(clips):
        for u in range(2):
            mine = lax.dynamic_index_in_dim(
                blocks, (core ^ u) * clips + (clip ^ w), 1, keepdims=False
            )
            if u or w:
                pairs = [
                    (s * clips + x, (s ^ u) * clips + (x ^ w))
                    for s in range(count)
                    for x in range(clips)
                ]
                mine = lax.ppermute(mine, ("seq", "dp"), pairs)
            lefts.append(mine.reshape(count // 2 * span, rows))
        far = right if w == 0 else swap(right, "dp", w)
        rights.extend([far, swap(far, "seq", 1)])
    total = 0.0
    for a in range(0, len(lefts), 2):
        left = jnp.concatenate(lefts[a : a + 2], axis=1)
        total = total + jnp.dot(
            left, jnp.concatenate(rights[a : a + 2], axis=0), preferred_element_type=F32
        )
    total = total.reshape(count // 2, span, right.shape[1])
    step = 2
    while total.shape[0] > 1:
        halves = total.reshape(total.shape[0] // 2, 2, span, right.shape[1])
        odd = (seq // step) % 2
        keep = lax.dynamic_index_in_dim(halves, odd, 1, keepdims=False)
        send = lax.dynamic_index_in_dim(halves, 1 - odd, 1, keepdims=False).astype(BF)
        total = keep + swap(send, "seq", step).astype(F32)
        step *= 2
    return total[0]


def on_device(
    latents, grad_out, sync_mod, w_qkv, w_out, q_gain, k_gain, frame_of, group_id, clip_len
):
    latents, grad_out, sync_mod = latents[0], grad_out[0], sync_mod[0]
    frame_of, group_id, clip_len = frame_of[0], group_id[0], clip_len[0]
    row_count, width_part = latents.shape
    frame_count = sync_mod.shape[0]
    model_width = sync_mod.shape[1] // 2
    heads, head_dim = q_gain.shape
    inner_width = heads * head_dim
    count = lax.axis_size("seq")
    sharers = count // heads
    seq = lax.axis_index("seq")
    head, part = seq // sharers, seq % sharers
    model_place = lax.axis_index("mp")

    inputs = full_width(latents)
    upstream = full_width(grad_out)

    back = max(
        frame_count * j - (FRAME_UP * row_count * j) // FRAME_DOWN for j in range(count)
    )
    back = min(frame_count, round_up(max(back, 1), 16))
    earlier = lax.ppermute(
        sync_mod[frame_count - back :], "seq", [(i, i + 1) for i in range(count - 1)]
    )
    window = jnp.concatenate([earlier, sync_mod], axis=0)
    local_frame = frame_of - (seq * frame_count - back)
    selector = (
        local_frame[:, None] == lax.iota(jnp.int32, frame_count + back)[None, :]
    ).astype(BF)
    modulation = jnp.dot(selector, window, preferred_element_type=F32)
    mod_scale = modulation[:, :model_width]
    mod_gate = modulation[:, model_width:]

    inputs_f = inputs.astype(F32)
    inv_norm = inv_rms(inputs_f)
    normed = inputs_f * inv_norm
    hidden = (normed * (1.0 + mod_scale)).astype(BF)
    flat_weight = w_qkv.reshape(model_width, 3 * inner_width)
    projected = jnp.dot(hidden, flat_weight, preferred_element_type=F32)
    projected = projected.reshape(row_count, 3, heads, head_dim)
    query_raw, key_raw = projected[:, 0], projected[:, 1]
    query_inv, key_inv = inv_rms(query_raw), inv_rms(key_raw)
    query_norm = (query_raw * query_inv * q_gain).astype(BF)
    key_norm = (key_raw * key_inv * k_gain).astype(BF)
    values = projected[:, 2].astype(BF)

    qkv = [
        jnp.stack([query_norm[:, j], key_norm[:, j], values[:, j]], axis=0) for j in range(heads)
    ]
    qkv = unxor(qkv, head)
    own = [qkv[0]] + [swap(qkv[t], "seq", t * sharers) for t in range(1, heads)]
    shared = [swap(own[t][1:], "seq", u) for t in range(heads) for u in range(1, sharers)]

    grad_attn = (upstream.astype(F32) * mod_gate).astype(BF)
    grad_heads = jnp.einsum("td,id->ti", grad_attn, w_out, preferred_element_type=F32)
    grad_heads = grad_heads.astype(BF)
    ups = unxor([grad_heads[:, j * head_dim : (j + 1) * head_dim] for j in range(heads)], head)
    ups = [ups[0]] + [swap(ups[t], "seq", t * sharers) for t in range(1, heads)]

    outs, key_grads = attention(head, part, group_id, clip_len, own, shared, ups)
    back_out, back_key = [], []
    for t in range(heads):
        total = key_grads[t][0]
        for u in range(1, sharers):
            total = total + swap(key_grads[t][u], "seq", u).astype(F32)
        if t:
            back_out.append(swap(outs[t], "seq", t * sharers))
            back_key.append(swap(total.astype(BF), "seq", t * sharers))
        else:
            back_out.append(outs[t])
            back_key.append(total.astype(BF))
    back_out, back_key = unxor(back_out, head), unxor(back_key, head)
    out_rows = jnp.concatenate([b[0] for b in back_out], axis=1)
    grad_qnorm = jnp.stack([b[1] for b in back_out], axis=1).astype(F32)
    grad_knorm = jnp.stack([b[0] for b in back_key], axis=1).astype(F32)
    grad_values = jnp.stack([b[1] for b in back_key], axis=1)

    attn_part = jnp.dot(out_rows, w_out, preferred_element_type=F32)
    attn_mine = width_sum(attn_part, width_part)
    gate_mine = lax.dynamic_slice_in_dim(mod_gate, model_place * width_part, width_part, 1)
    mixed = (latents.astype(F32) + gate_mine * attn_mine).astype(BF)

    grad_query = norm_back(query_raw, query_inv, q_gain, grad_qnorm).astype(BF)
    grad_key = norm_back(key_raw, key_inv, k_gain, grad_knorm).astype(BF)
    grad_proj = jnp.concatenate(
        [g.reshape(row_count, inner_width) for g in (grad_query, grad_key, grad_values)], axis=1
    )

    grad_wout = weight_grad(jnp.transpose(grad_attn), out_rows)
    grad_wqkv = weight_grad(jnp.transpose(hidden), grad_proj)

    grad_hidden = jnp.einsum("tf,ef->te", grad_proj, flat_weight, preferred_element_type=F32)
    full_dot = jnp.sum(grad_hidden * (1.0 + mod_scale) * normed, axis=-1, keepdims=True)
    part_dot = full_dot
    full_dot = sum(
        [swap(part_dot, "mp", t) for t in range(1, lax.axis_size("mp"))], part_dot
    )
    grad_mine = width_sum(grad_hidden, width_part)
    scale_mine = lax.dynamic_slice_in_dim(mod_scale, model_place * width_part, width_part, 1)
    normed_mine = latents.astype(F32) * inv_norm
    grad_normed = grad_mine * (1.0 + scale_mine)
    grad_inputs = inv_norm * (grad_normed - normed_mine * (full_dot / model_width))
    grad_latents = (grad_out.astype(F32) + grad_inputs).astype(BF)
    return (
        mixed[None],
        grad_latents[None],
        grad_wqkv.reshape(-1, 3, inner_width),
        jnp.transpose(grad_wout),
    )


def solution(mesh):
    in_specs = (
        P("dp", "seq", "mp"),
        P("dp", "seq", "mp"),
        P("dp", "seq", None),
        P(None, None, "mp"),
        P("mp", None),
        P("mp", None),
        P("mp", None),
        P("dp", "seq"),
        P("dp", None),
        P("dp"),
    )
    out_specs = (
        P("dp", "seq", "mp"),
        P("dp", "seq", "mp"),
        P(("seq", "dp"), None, "mp"),
        P("mp", ("seq", "dp")),
    )
    return jax.shard_map(
        on_device, mesh=mesh, in_specs=in_specs, out_specs=out_specs, check_vma=False
    )
```

```python
import functools
import math

import jax
import jax.numpy as jnp
from jax import lax
from jax.experimental import pallas as pl
from jax.experimental.pallas import tpu as pltpu
from jax.sharding import PartitionSpec as P

EPSILON = 1e-06
NEG_FILL = -1e30
GROUP_MOST = 96
FRAME_UP, FRAME_DOWN = 96, 125
NO_GROUP = 1 << 30
LANES = 128
BF = jnp.bfloat16
F32 = jnp.float32
ANY = pl.BlockSpec(memory_space=pl.ANY)
VMEM = pl.BlockSpec(memory_space=pltpu.VMEM)
SMEM = pl.BlockSpec(memory_space=pltpu.SMEM)
OVER_LAST = (((1,), (1,)), ((), ()))
OVER_FIRST = (((0,), (0,)), ((), ()))


def swap(value, axis, distance):
    count = lax.axis_size(axis)
    return lax.ppermute(value, axis, [(i, i ^ distance) for i in range(count)])


def unxor(pieces, place):
    pieces = list(pieces)
    for bit in range((len(pieces) - 1).bit_length()):
        odd = ((place >> bit) & 1) == 1
        pieces = [jnp.where(odd, pieces[j ^ (1 << bit)], pieces[j]) for j in range(len(pieces))]
    return pieces


def inv_rms(values):
    return lax.rsqrt(jnp.mean(values * values, axis=-1, keepdims=True) + EPSILON)


def norm_back(raw, gains, upstream):
    inv_norm = inv_rms(raw)
    inner_dot = jnp.mean(upstream * gains * raw, axis=-1, keepdims=True)
    return inv_norm * (gains * upstream - raw * inv_norm * inv_norm * inner_dot)


def round_up(value, step):
    return -(-value // step) * step


class Copies:
    def __init__(self, sems):
        self.sems, self.made = sems, []

    def start(self, source, target):
        copy = pltpu.make_async_copy(source, target, self.sems.at[len(self.made)])
        copy.start()
        self.made.append(copy)
        return copy

    def wait(self):
        for copy in self.made:
            copy.wait()


def call(kernel, name, out, specs, args, scratch, copies, mib, flops, out_specs=None):
    results = pl.pallas_call(
        kernel,
        out_shape=[jax.ShapeDtypeStruct(*o) for o in out],
        in_specs=specs,
        out_specs=out_specs or [ANY] * len(out),
        scratch_shapes=scratch + [pltpu.SemaphoreType.DMA((copies,))],
        compiler_params=pltpu.CompilerParams(vmem_limit_bytes=mib << 20),
        cost_estimate=pl.CostEstimate(flops=flops, bytes_accessed=2 << 20, transcendentals=0),
        name=name,
    )(*args)
    return list(results)


def spread(place, pieces, target, copies):
    width = pieces[0].shape[-1]
    for t, piece in enumerate(pieces):
        if len(pieces) == 1:
            columns = slice(None)
        else:
            columns = pl.ds(pl.multiple_of((place ^ t) * width, LANES), width)
        copies.start(piece, target.at[:, columns])


def width_pieces(value):
    pieces = [value] + [swap(value, "mp", t) for t in range(1, lax.axis_size("mp"))]
    if value.shape[-1] % LANES:
        return [jnp.concatenate(unxor(pieces, lax.axis_index("mp")), axis=-1)]
    return pieces


def width_outs(rows, width, width_part):
    if width_part % LANES:
        return [((rows, width), F32)]
    others = width // width_part - 1
    return [((rows, width_part), F32)] + [((rows, width_part), BF)] * others


def write_width(place, source, refs):
    if len(refs) == 1:
        refs[0][...] = source[...]
        return
    width = refs[0].shape[-1]
    for t, ref in enumerate(refs):
        columns = pl.ds(pl.multiple_of((place ^ t) * width, LANES), width)
        ref[...] = source[:, columns].astype(ref.dtype)


def width_sum(parts, width_part):
    place = lax.axis_index("mp")
    count = lax.axis_size("mp")
    if width_part % LANES:
        whole = parts[0]
        parts = [
            lax.dynamic_slice_in_dim(whole, (place ^ t) * width_part, width_part, 1)
            for t in range(count)
        ]
    total = parts[0]
    for t in range(1, count):
        total = total + swap(parts[t].astype(BF), "mp", t).astype(F32)
    return total


def project_kernel(heads, width_count, *refs):
    place_ref, q_gain_ref, k_gain_ref, weight_ref, mod_ref = refs[:5]
    inputs = refs[5 : 5 + width_count]
    refs = refs[5 + width_count :]
    pieces = refs[:heads]
    hidden_ref, raw_ref, inv_ref, inputs_s, pieces_s, sems = refs[heads:]
    copies = Copies(sems)
    spread(place_ref[2], inputs, inputs_s, copies)
    copies.wait()
    model_width = inputs_s.shape[1]
    values = inputs_s[...].astype(F32)
    inv_norm = inv_rms(values)
    inv_ref[...] = inv_norm
    scale = 1.0 + mod_ref[:, :model_width].astype(F32)
    hidden = (values * inv_norm * scale).astype(BF)
    hidden_ref[...] = hidden
    raw_ref[...] = jnp.dot(hidden, weight_ref[...], preferred_element_type=F32)
    inner = raw_ref.shape[1] // 3
    dim = inner // heads
    head = place_ref[0]
    for t in range(heads):
        own = head ^ t
        at = pl.multiple_of(own * dim, LANES)
        query = raw_ref[:, pl.ds(at, dim)]
        key = raw_ref[:, pl.ds(at + inner, dim)]
        q_gain = q_gain_ref[pl.ds(own, 1), :]
        k_gain = k_gain_ref[pl.ds(own, 1), :]
        pieces_s[t, 0] = (query * inv_rms(query) * q_gain).astype(BF)
        pieces_s[t, 1] = (key * inv_rms(key) * k_gain).astype(BF)
        pieces_s[t, 2] = raw_ref[:, pl.ds(at + 2 * inner, dim)].astype(BF)
        copies.start(pieces_s.at[t], pieces[t])
    for copy in copies.made[width_count:]:
        copy.wait()


def upstream_kernel(heads, width_count, *refs):
    place_ref, weight_ref, mod_ref = refs[:3]
    upstream = refs[3 : 3 + width_count]
    refs = refs[3 + width_count :]
    pieces = refs[:heads]
    grad_ref, upstream_s, heads_s, sems = refs[heads:]
    copies = Copies(sems)
    spread(place_ref[2], upstream, upstream_s, copies)
    copies.wait()
    model_width = upstream_s.shape[1]
    grad = (upstream_s[...].astype(F32) * mod_ref[:, model_width:].astype(F32)).astype(BF)
    grad_ref[...] = grad
    heads_s[...] = lax.dot_general(
        grad, weight_ref[...], OVER_LAST, preferred_element_type=F32
    ).astype(BF)
    dim = heads_s.shape[1] // heads
    for t in range(heads):
        columns = pl.ds(pl.multiple_of((place_ref[0] ^ t) * dim, LANES), dim)
        copies.start(heads_s.at[:, columns], pieces[t])
    for copy in copies.made[width_count:]:
        copy.wait()


def turn_kernel(blocks, clips, *refs):
    place_ref, hidden_ref, grad_ref = refs[:3]
    pieces = refs[3 : 3 + 2 * clips]
    turned_s, sems = refs[3 + 2 * clips :]
    span = turned_s.shape[-2]
    for at, ref in enumerate((hidden_ref, grad_ref)):
        turned = jnp.transpose(ref[...].astype(F32))
        for b in range(blocks * 2 * clips):
            turned_s[at, b // (2 * clips), b % (2 * clips)] = turned[
                b * span : (b + 1) * span
            ].astype(BF)
    copies = Copies(sems)
    for u in range(2):
        for w in range(clips):
            own = (place_ref[3] ^ u) * clips + (place_ref[4] ^ w)
            copies.start(turned_s.at[:, :, own], pieces[u * clips + w])
    copies.wait()


def attention_kernel(heads, sharers, rows, block, factor, *refs):
    place_ref, key_group_ref, query_group_ref = refs[:3]
    at = 3
    own = refs[at : at + heads]
    at += heads
    shared = refs[at : at + heads * (sharers - 1)]
    at += heads * (sharers - 1)
    ups = refs[at : at + heads]
    at += heads
    outs = refs[at : at + heads]
    at += heads
    key_grads = refs[at : at + heads * sharers]
    at += heads * sharers
    key_s, value_s, query_s, up_s, out_s, dk_s, dv_s, half_s, sems = refs[at:]
    head = place_ref[0]
    part = place_ref[1]
    dim = key_s.shape[-1]
    span = heads * sharers * rows
    total = heads * rows
    copies = Copies(sems)
    for t in range(heads):
        m = head ^ t
        copies.start(own[t].at[0], query_s.at[m])
        copies.start(own[t].at[1], key_s.at[m * sharers + part])
        copies.start(own[t].at[2], value_s.at[m * sharers + part])
        for u in range(1, sharers):
            piece = shared[t * (sharers - 1) + u - 1]
            copies.start(piece.at[0], key_s.at[m * sharers + (part ^ u)])
            copies.start(piece.at[1], value_s.at[m * sharers + (part ^ u)])
        copies.start(ups[t], up_s.at[m])
    dk_s[...] = jnp.zeros_like(dk_s)
    dv_s[...] = jnp.zeros_like(dv_s)
    group_col = jnp.transpose(jnp.broadcast_to(key_group_ref[...], (128, span)))
    group_col = jnp.concatenate([group_col] * (-(-block // 128)), axis=1)[:, :block]
    copies.wait()
    loaded = len(copies.made)
    keys = key_s[...].reshape(span, dim)
    values = value_s[...].reshape(span, dim)
    queries = query_s[...].reshape(total, dim)
    upstream = up_s[...].reshape(total, dim)
    scale = factor * math.log2(math.e)
    for j in range(total // block):
        last = ((j + 1) * block - 1) // rows
        reach = min(span, round_up((last + 1) * sharers * rows + GROUP_MOST - 1, 128))
        lanes = slice(j * block, (j + 1) * block)
        query = queries[lanes]
        up = upstream[lanes]
        key = keys[:reach]
        value = values[:reach]
        logits = lax.dot_general(key, query, OVER_LAST, preferred_element_type=F32)
        logits = jnp.where(group_col[:reach] <= query_group_ref[:, lanes], logits, NEG_FILL)
        row_max = jnp.max(logits, axis=0, keepdims=True)
        unnorm = jnp.exp2((logits - row_max) * scale)
        inverse = 1.0 / jnp.sum(unnorm, axis=0, keepdims=True)
        out = lax.dot_general(value, unnorm.astype(BF), OVER_FIRST, preferred_element_type=F32)
        out = (out * inverse).astype(BF)
        up_t = jnp.transpose(up.astype(F32))
        out_dot = jnp.sum(up_t * out.astype(F32), axis=0, keepdims=True)
        probs = unnorm * inverse
        grad_probs = lax.dot_general(value, up, OVER_LAST, preferred_element_type=F32)
        grad_logits = (probs * (grad_probs - out_dot)).astype(BF)
        grad_query = lax.dot_general(key, grad_logits, OVER_FIRST, preferred_element_type=F32)
        out_s[0, lanes, :] = jnp.transpose(out.astype(F32)).astype(BF)
        out_s[1, lanes, :] = jnp.transpose(grad_query * factor).astype(BF)
        dk_s[:reach, :] += jnp.dot(grad_logits, query, preferred_element_type=F32)
        dv_s[:reach, :] += jnp.dot(probs.astype(BF), up, preferred_element_type=F32)
    for t in range(heads):
        m = head ^ t
        for u in range(sharers):
            there = pl.ds(pl.multiple_of((m * sharers + (part ^ u)) * rows, 64), rows)
            ref = key_grads[t * sharers + u]
            if u == 0:
                copies.start(dk_s.at[there, :], ref.at[0])
                copies.start(dv_s.at[there, :], ref.at[1])
            else:
                slot = half_s.at[t * (sharers - 1) + u - 1]
                slot[0] = dk_s[there, :].astype(BF)
                slot[1] = dv_s[there, :].astype(BF)
                copies.start(slot, ref)
        here = pl.ds(pl.multiple_of(m * rows, 64), rows)
        copies.start(out_s.at[:, here, :], outs[t])
    for copy in copies.made[loaded:]:
        copy.wait()


def attention(place, part, group_ids, clip_length, own, shared, ups):
    heads = len(own)
    sharers = len(shared) // heads + 1
    rows, width = ups[0].shape
    span = heads * sharers * rows
    total = heads * rows
    block = 256 if total % 256 == 0 else total
    positions = lax.iota(jnp.int32, span)
    key_group = jnp.where(positions < clip_length, group_ids, NO_GROUP)[None, :]
    query_group = lax.dynamic_index_in_dim(
        group_ids.reshape(heads, sharers, rows), part, 1, keepdims=False
    ).reshape(1, total)
    pair = (2, rows, width)
    out = [(pair, BF)] * heads
    for _ in range(heads):
        out.append((pair, F32))
        out.extend([(pair, BF)] * (sharers - 1))
    loads = heads * (4 + 2 * (sharers - 1))
    stores = heads * (3 + sharers - 1)
    got = call(
        functools.partial(attention_kernel, heads, sharers, rows, block, width ** (-0.5)),
        "attention",
        out,
        [SMEM, VMEM, VMEM] + [ANY] * (2 * heads + heads * (sharers - 1)),
        [place, key_group, query_group, *own, *shared, *ups],
        [
            pltpu.VMEM((heads * sharers, rows, width), BF),
            pltpu.VMEM((heads * sharers, rows, width), BF),
            pltpu.VMEM((heads, rows, width), BF),
            pltpu.VMEM((heads, rows, width), BF),
            pltpu.VMEM((2, total, width), BF),
            pltpu.VMEM((span, width), F32),
            pltpu.VMEM((span, width), F32),
            pltpu.VMEM((max(1, heads * (sharers - 1)),) + pair, BF),
        ],
        loads + stores,
        40,
        12 * total * span * width,
    )
    outs = got[:heads]
    key_grads = [got[heads + t * sharers : heads + (t + 1) * sharers] for t in range(heads)]
    return outs, key_grads


def share_kernel(heads, sharers, factor, *refs):
    terms = refs[: heads * sharers]
    sums = refs[heads * sharers : heads * sharers + heads]
    own_s, others_s, sums_s, sems = refs[heads * sharers + heads :]
    copies = Copies(sems)
    for t in range(heads):
        copies.start(terms[t * sharers], own_s.at[t])
        for u in range(1, sharers):
            copies.start(terms[t * sharers + u], others_s.at[t * (sharers - 1) + u - 1])
    copies.wait()
    loaded = len(copies.made)
    for t in range(heads):
        total = own_s[t]
        for u in range(1, sharers):
            total = total + others_s[t * (sharers - 1) + u - 1].astype(F32)
        sums_s[t, 0] = (total[0] * factor).astype(BF)
        sums_s[t, 1] = total[1].astype(BF)
        copies.start(sums_s.at[t], sums[t])
    for copy in copies.made[loaded:]:
        copy.wait()


def query_kernel(heads, *refs):
    place_ref, gain_ref, raw_ref = refs[:3]
    pieces = refs[3 : 3 + heads]
    rows_ref, grad_ref, pieces_s, sems = refs[3 + heads :]
    copies = Copies(sems)
    for t in range(heads):
        copies.start(pieces[t], pieces_s.at[t])
    copies.wait()
    dim = pieces_s.shape[-1]
    for t in range(heads):
        own = place_ref[0] ^ t
        columns = pl.ds(pl.multiple_of(own * dim, LANES), dim)
        rows_ref[:, columns] = pieces_s[t, 0]
        grad_ref[:, columns] = norm_back(
            raw_ref[:, columns], gain_ref[pl.ds(own, 1), :], pieces_s[t, 1].astype(F32)
        ).astype(BF)


def key_kernel(heads, *refs):
    place_ref, gain_ref, raw_ref = refs[:3]
    pieces = refs[3 : 3 + heads]
    key_ref, value_ref, pieces_s, sems = refs[3 + heads :]
    copies = Copies(sems)
    for t in range(heads):
        copies.start(pieces[t], pieces_s.at[t])
    copies.wait()
    dim = pieces_s.shape[-1]
    inner = heads * dim
    for t in range(heads):
        own = place_ref[0] ^ t
        at = pl.multiple_of(own * dim, LANES)
        columns = pl.ds(at, dim)
        key_ref[:, columns] = norm_back(
            raw_ref[:, pl.ds(at + inner, dim)],
            gain_ref[pl.ds(own, 1), :],
            pieces_s[t, 0].astype(F32),
        ).astype(BF)
        value_ref[:, columns] = pieces_s[t, 1]


def mix_kernel(place_ref, rows_ref, weight_ref, *refs):
    whole_s = refs[-2]
    whole_s[...] = jnp.dot(rows_ref[...], weight_ref[...], preferred_element_type=F32)
    write_width(place_ref[2], whole_s, refs[:-2])


def hidden_kernel(width_count, *refs):
    place_ref, grads, weight_ref, mod_ref, inv_ref = refs[0], refs[1:4], *refs[4:7]
    inputs = refs[7 : 7 + width_count]
    dot_ref = refs[7 + width_count]
    outs = refs[8 + width_count : -3]
    whole_s, inputs_s, sems = refs[-3:]
    copies = Copies(sems)
    spread(place_ref[2], inputs, inputs_s, copies)
    inner = grads[0].shape[1]
    total = 0.0
    for at, grad in enumerate(grads):
        total = total + lax.dot_general(
            grad[...],
            weight_ref[:, at * inner : (at + 1) * inner],
            OVER_LAST,
            preferred_element_type=F32,
        )
    whole_s[...] = total
    copies.wait()
    write_width(place_ref[2], whole_s, outs)
    model_width = inputs_s.shape[1]
    scale = 1.0 + mod_ref[:, :model_width].astype(F32)
    normed = inputs_s[...].astype(F32) * inv_ref[...]
    dot = jnp.sum(whole_s[...] * scale * normed, axis=1, keepdims=True)
    turned = jnp.transpose(jnp.broadcast_to(dot, (dot.shape[0], LANES)))
    dot_ref[...] = turned[:8]


def outer_kernel(step, *refs):
    place_ref = refs[0]
    count = (len(refs) - 4) // 2
    lefts, rights = refs[1 : 1 + count], refs[1 + count : 1 + 2 * count]
    send_ref, keep_ref, _ = refs[1 + 2 * count :]
    blocks, span, rows = lefts[0].shape
    total = 0.0
    for left, right in zip(lefts, rights):
        total = total + jnp.dot(
            left[...].reshape(blocks * span, rows), right[...], preferred_element_type=F32
        )
    total = total.reshape(blocks, span, total.shape[1])
    odd = (place_ref[5] // step) % 2
    for b in range(blocks // 2):
        first, second = total[2 * b], total[2 * b + 1]
        keep_ref[b] = jnp.where(odd == 1, second, first)
        send_ref[b] = jnp.where(odd == 1, first, second).astype(BF)


def gathered(right):
    rights = []
    for w in range(lax.axis_size("dp")):
        far = right if w == 0 else swap(right, "dp", w)
        rights.append(far)
    return rights + [swap(far, "seq", 1) for far in rights]


def weight_grad(place, lefts, right, seq):
    rights = gathered(right)
    blocks, span, rows = lefts[0].shape
    width = right.shape[1]
    half = (blocks // 2, span, width)
    send, keep = call(
        functools.partial(outer_kernel, 2),
        "weight_sum",
        [(half, BF), (half, F32)],
        [SMEM] + [VMEM] * (2 * len(lefts)),
        [place, *lefts, *rights],
        [],
        1,
        24,
        2 * blocks * span * rows * width * len(lefts),
        [VMEM, VMEM],
    )
    step = 2
    while True:
        total = keep + swap(send, "seq", step).astype(F32)
        step *= 2
        if total.shape[0] == 1:
            return total[0]
        halves = total.reshape(total.shape[0] // 2, 2, span, width)
        odd = (seq // step) % 2
        keep = lax.dynamic_index_in_dim(halves, odd, 1, keepdims=False)
        send = lax.dynamic_index_in_dim(halves, 1 - odd, 1, keepdims=False).astype(BF)


def on_device(
    latents, grad_out, sync_mod, w_qkv, w_out, q_gain, k_gain, frame_of, group_id, clip_len
):
    latents, grad_out, sync_mod = latents[0], grad_out[0], sync_mod[0]
    frame_of, group_id, clip_len = frame_of[0], group_id[0], clip_len[0]
    rows, width_part = latents.shape
    frame_count = sync_mod.shape[0]
    model_width = sync_mod.shape[1] // 2
    heads, head_dim = q_gain.shape
    inner = heads * head_dim
    count, clips = lax.axis_size("seq"), lax.axis_size("dp")
    sharers = count // heads
    seq, clip = lax.axis_index("seq"), lax.axis_index("dp")
    head, part = seq // sharers, seq % sharers
    model_place = lax.axis_index("mp")
    place = jnp.stack([head, part, model_place, seq % 2, clip, seq]).astype(jnp.int32)

    inputs = width_pieces(latents)
    upstream = width_pieces(grad_out)
    width_count = len(inputs)

    back = max(frame_count * j - (FRAME_UP * rows * j) // FRAME_DOWN for j in range(count))
    back = min(frame_count, round_up(max(back, 1), 16))
    earlier = lax.ppermute(
        sync_mod[frame_count - back :], "seq", [(i, i + 1) for i in range(count - 1)]
    )
    window = jnp.concatenate([earlier, sync_mod], axis=0)
    local_frame = frame_of - (seq * frame_count - back)
    selector = (
        local_frame[:, None] == lax.iota(jnp.int32, frame_count + back)[None, :]
    ).astype(BF)
    mod = jnp.dot(selector, window, preferred_element_type=F32).astype(BF)

    weight = w_qkv.reshape(model_width, 3 * inner)
    got = call(
        functools.partial(project_kernel, heads, width_count),
        "project",
        [((3, rows, head_dim), BF)] * heads
        + [((rows, model_width), BF), ((rows, 3 * inner), F32), ((rows, 1), F32)],
        [SMEM] + [VMEM] * 4 + [ANY] * width_count,
        [place, q_gain, k_gain, weight, mod, *inputs],
        [pltpu.VMEM((rows, model_width), BF), pltpu.VMEM((heads, 3, rows, head_dim), BF)],
        width_count + heads,
        32,
        6 * rows * model_width * inner,
        [ANY] * heads + [VMEM] * 3,
    )
    own, (hidden, raw, inv_norm) = got[:heads], got[heads:]
    own = [own[0]] + [swap(own[t], "seq", t * sharers) for t in range(1, heads)]
    shared = [swap(own[t][1:], "seq", u) for t in range(heads) for u in range(1, sharers)]

    got = call(
        functools.partial(upstream_kernel, heads, width_count),
        "upstream",
        [((rows, head_dim), BF)] * heads + [((rows, model_width), BF)],
        [SMEM] + [VMEM] * 2 + [ANY] * width_count,
        [place, w_out, mod, *upstream],
        [pltpu.VMEM((rows, model_width), BF), pltpu.VMEM((rows, inner), BF)],
        width_count + heads,
        24,
        2 * rows * model_width * inner,
        [ANY] * heads + [VMEM],
    )
    ups, grad_attn = got[:heads], got[heads]
    ups = [ups[0]] + [swap(ups[t], "seq", t * sharers) for t in range(1, heads)]

    blocks = count // 2
    span = model_width // (count * clips)
    lefts = call(
        functools.partial(turn_kernel, blocks, clips),
        "turn",
        [((2, blocks, span, rows), BF)] * (2 * clips),
        [SMEM, VMEM, VMEM],
        [place, hidden, grad_attn],
        [pltpu.VMEM((2, blocks, 2 * clips, span, rows), BF)],
        2 * clips,
        24,
        1 << 28,
    )
    for u in range(2):
        for w in range(clips):
            if u or w:
                pairs = [
                    (s * clips + x, (s ^ u) * clips + (x ^ w))
                    for s in range(count)
                    for x in range(clips)
                ]
                lefts[u * clips + w] = lax.ppermute(lefts[u * clips + w], ("seq", "dp"), pairs)

    outs, key_grads = attention(place, part, group_id, clip_len, own, shared, ups)
    terms = []
    for t in range(heads):
        terms.append(key_grads[t][0])
        terms.extend(swap(key_grads[t][u], "seq", u) for u in range(1, sharers))
    pair = (2, rows, head_dim)
    sums = call(
        functools.partial(share_kernel, heads, sharers, head_dim ** (-0.5)),
        "share",
        [(pair, BF)] * heads,
        [ANY] * len(terms),
        terms,
        [
            pltpu.VMEM((heads,) + pair, F32),
            pltpu.VMEM((max(1, heads * (sharers - 1)),) + pair, BF),
            pltpu.VMEM((heads,) + pair, BF),
        ],
        heads * sharers + heads,
        16,
        1 << 24,
    )
    back_out = [outs[0]] + [swap(outs[t], "seq", t * sharers) for t in range(1, heads)]
    back_key = [sums[0]] + [swap(sums[t], "seq", t * sharers) for t in range(1, heads)]
    out_rows, grad_query = call(
        functools.partial(query_kernel, heads),
        "query_back",
        [((rows, inner), BF)] * 2,
        [SMEM, VMEM, VMEM] + [ANY] * heads,
        [place, q_gain, raw, *back_out],
        [pltpu.VMEM((heads,) + pair, BF)],
        heads,
        16,
        1 << 24,
        [VMEM] * 2,
    )
    grad_key, grad_value = call(
        functools.partial(key_kernel, heads),
        "key_back",
        [((rows, inner), BF)] * 2,
        [SMEM, VMEM, VMEM] + [ANY] * heads,
        [place, k_gain, raw, *back_key],
        [pltpu.VMEM((heads,) + pair, BF)],
        heads,
        16,
        1 << 24,
        [VMEM] * 2,
    )

    parts = call(
        mix_kernel,
        "mix",
        width_outs(rows, model_width, width_part),
        [SMEM, VMEM, VMEM],
        [place, out_rows, w_out],
        [pltpu.VMEM((rows, model_width), F32)],
        1,
        24,
        2 * rows * model_width * inner,
        [VMEM] * len(width_outs(rows, model_width, width_part)),
    )
    attn_mine = width_sum(parts, width_part)
    gate_mine = lax.dynamic_slice_in_dim(
        mod, model_width + model_place * width_part, width_part, 1
    )
    mixed = (latents.astype(F32) + gate_mine.astype(F32) * attn_mine).astype(BF)

    got = call(
        functools.partial(hidden_kernel, width_count),
        "hidden_back",
        [((8, rows), F32)] + width_outs(rows, model_width, width_part),
        [SMEM] + [VMEM] * 6 + [ANY] * width_count,
        [place, grad_query, grad_key, grad_value, weight, mod, inv_norm, *inputs],
        [pltpu.VMEM((rows, model_width), F32), pltpu.VMEM((rows, model_width), BF)],
        width_count,
        40,
        6 * rows * model_width * inner,
        [VMEM] * (1 + len(width_outs(rows, model_width, width_part))),
    )
    part_dot, parts = got[0], got[1:]
    full_dot = part_dot
    for t in range(1, lax.axis_size("mp")):
        full_dot = full_dot + swap(part_dot, "mp", t)
    grad_mine = width_sum(parts, width_part)
    scale_mine = lax.dynamic_slice_in_dim(mod, model_place * width_part, width_part, 1)
    normed_mine = latents.astype(F32) * inv_norm
    grad_normed = grad_mine * (1.0 + scale_mine.astype(F32))
    inner_mean = full_dot[0][:, None] / model_width
    grad_inputs = inv_norm * (grad_normed - normed_mine * inner_mean)
    grad_latents = (grad_out.astype(F32) + grad_inputs).astype(BF)

    left_hidden = [left[0] for left in lefts]
    left_grad = [left[1] for left in lefts]
    grad_wout = weight_grad(place, left_grad, out_rows, seq)
    grad_wqkv = jnp.stack(
        [weight_grad(place, left_hidden, g, seq) for g in (grad_query, grad_key, grad_value)],
        axis=1,
    )
    return mixed[None], grad_latents[None], grad_wqkv, jnp.transpose(grad_wout)


def solution(mesh):
    in_specs = (
        P("dp", "seq", "mp"),
        P("dp", "seq", "mp"),
        P("dp", "seq", None),
        P(None, None, "mp"),
        P("mp", None),
        P("mp", None),
        P("mp", None),
        P("dp", "seq"),
        P("dp", None),
        P("dp"),
    )
    out_specs = (
        P("dp", "seq", "mp"),
        P("dp", "seq", "mp"),
        P(("seq", "dp"), None, "mp"),
        P("mp", ("seq", "dp")),
    )
    return jax.shard_map(
        on_device, mesh=mesh, in_specs=in_specs, out_specs=out_specs, check_vma=False
    )
```

```python
import functools
import math

import jax
import jax.numpy as jnp
from jax import lax
from jax.experimental import pallas as pl
from jax.experimental.pallas import tpu as pltpu
from jax.sharding import PartitionSpec as P

EPSILON = 1e-06
NEG_FILL = -1e30
GROUP_MOST = 96
FRAME_UP, FRAME_DOWN = 96, 125
NO_GROUP = 1 << 30
ATTENTION_MIB = 24
LANES = 128
BF = jnp.bfloat16
F32 = jnp.float32
ANY = pl.BlockSpec(memory_space=pl.ANY)
HBM = pl.BlockSpec(memory_space=pltpu.HBM)
VMEM = pl.BlockSpec(memory_space=pltpu.VMEM)
OVER_LAST = (((1,), (1,)), ((), ()))
OVER_FIRST = (((0,), (0,)), ((), ()))


def swap(value, axis, distance):
    count = lax.axis_size(axis)
    return lax.ppermute(value, axis, [(i, i ^ distance) for i in range(count)])


def unxor(pieces, place):
    pieces = list(pieces)
    for bit in range((len(pieces) - 1).bit_length()):
        odd = ((place >> bit) & 1) == 1
        pieces = [jnp.where(odd, pieces[j ^ (1 << bit)], pieces[j]) for j in range(len(pieces))]
    return pieces


def inv_rms(values):
    return lax.rsqrt(jnp.mean(values * values, axis=-1, keepdims=True) + EPSILON)


def norm_back(raw, gains, upstream):
    inv_norm = inv_rms(raw)
    inner_dot = jnp.mean(upstream * gains * raw, axis=-1, keepdims=True)
    return inv_norm * (gains * upstream - raw * inv_norm * inv_norm * inner_dot)


def round_up(value, step):
    return -(-value // step) * step


def head_place(heads):
    sharers = lax.axis_size("seq") // heads
    seq = lax.axis_index("seq")
    return seq // sharers, seq % sharers


def call(kernel, name, out, args, scratch, mib, flops, after=(), specs=None, copies=0):
    given, late = len(args), len(after)

    def body(*refs):
        kernel(*refs[:given], *refs[given + late :])

    scratch = [pltpu.VMEM(*s) for s in scratch]
    if copies:
        scratch.append(pltpu.SemaphoreType.DMA((copies,)))
    return list(
        pl.pallas_call(
            body,
            out_shape=[jax.ShapeDtypeStruct(*o) for o in out],
            in_specs=(specs or [VMEM] * given) + [ANY] * late,
            out_specs=[VMEM] * len(out),
            scratch_shapes=scratch,
            compiler_params=pltpu.CompilerParams(vmem_limit_bytes=mib << 20),
            cost_estimate=pl.CostEstimate(flops=flops, bytes_accessed=1 << 20, transcendentals=0),
            name=name,
        )(*args, *after)
    )


class Copies:
    def __init__(self, sems):
        self.sems, self.made = sems, []

    def start(self, source, target):
        copy = pltpu.make_async_copy(source, target, self.sems.at[len(self.made)])
        copy.start()
        self.made.append(copy)

    def wait(self):
        for copy in self.made:
            copy.wait()


def stage_kernel(count, *refs):
    copies = Copies(refs[-1])
    for source, target in zip(refs[:count], refs[count : 2 * count]):
        copies.start(source, target)
    copies.wait()


def columns_of(place, width):
    return pl.ds(pl.multiple_of(place * width, LANES), width)


def spread(pieces, target):
    place = lax.axis_index("mp")
    width = pieces[0].shape[-1]
    for t, piece in enumerate(pieces):
        if len(pieces) == 1:
            target[...] = piece[...]
        else:
            target[:, columns_of(place ^ t, width)] = piece[...]


def width_pieces(value):
    pieces = [value] + [swap(value, "mp", t) for t in range(1, lax.axis_size("mp"))]
    if value.shape[-1] % LANES:
        return [jnp.concatenate(unxor(pieces, lax.axis_index("mp")), axis=-1)]
    return pieces


def width_outs(rows, width, width_part):
    if width_part % LANES:
        return [((rows, width), F32)]
    others = width // width_part - 1
    return [((rows, width_part), F32)] + [((rows, width_part), BF)] * others


def write_width(source, refs):
    if len(refs) == 1:
        refs[0][...] = source[...]
        return
    place = lax.axis_index("mp")
    for t, ref in enumerate(refs):
        ref[...] = source[:, columns_of(place ^ t, ref.shape[-1])].astype(ref.dtype)


def width_sum(parts, width_part):
    place = lax.axis_index("mp")
    count = lax.axis_size("mp")
    if width_part % LANES:
        whole = parts[0]
        parts = [
            lax.dynamic_slice_in_dim(whole, (place ^ t) * width_part, width_part, 1)
            for t in range(count)
        ]
    total = parts[0]
    for t in range(1, count):
        total = total + swap(parts[t].astype(BF), "mp", t).astype(F32)
    return total


def project_kernel(heads, width_count, *refs):
    q_gain_ref, k_gain_ref, weight_ref, mod_ref = refs[:4]
    inputs = refs[4 : 4 + width_count]
    refs = refs[4 + width_count :]
    pieces = refs[:heads]
    hidden_ref, raw_ref, inv_ref, inputs_s, values_s = refs[heads:]
    spread(inputs, inputs_s)
    model_width = inputs_s.shape[1]
    values = inputs_s[...].astype(F32)
    inv_norm = inv_rms(values)
    inv_ref[...] = inv_norm
    scale = 1.0 + mod_ref[:, :model_width].astype(F32)
    hidden = (values * inv_norm * scale).astype(BF)
    hidden_ref[...] = hidden
    for at in range(2):
        raw_ref[at] = jnp.dot(hidden, weight_ref[at], preferred_element_type=F32)
    values_s[...] = jnp.dot(hidden, weight_ref[2], preferred_element_type=F32).astype(BF)
    dim = values_s.shape[1] // heads
    head, _ = head_place(heads)
    for t in range(heads):
        own = head ^ t
        columns = columns_of(own, dim)
        for at, gain_ref in enumerate((q_gain_ref, k_gain_ref)):
            raw = raw_ref[at, :, columns]
            pieces[t][at] = (raw * inv_rms(raw) * gain_ref[pl.ds(own, 1), :]).astype(BF)
        pieces[t][2] = values_s[:, columns]


def upstream_kernel(heads, width_count, *refs):
    weight_ref, mod_ref = refs[:2]
    upstream = refs[2 : 2 + width_count]
    refs = refs[2 + width_count :]
    pieces = refs[:heads]
    grad_ref, upstream_s, heads_s = refs[heads:]
    spread(upstream, upstream_s)
    model_width = upstream_s.shape[1]
    grad = (upstream_s[...].astype(F32) * mod_ref[:, model_width:].astype(F32)).astype(BF)
    grad_ref[...] = grad
    heads_s[...] = lax.dot_general(
        grad, weight_ref[...], OVER_LAST, preferred_element_type=F32
    ).astype(BF)
    dim = heads_s.shape[1] // heads
    head, _ = head_place(heads)
    for t in range(heads):
        pieces[t][...] = heads_s[:, columns_of(head ^ t, dim)]


def turn_kernel(blocks, clips, *refs):
    sources = refs[:2]
    pieces = refs[2 : 2 + 2 * clips]
    turned_s = refs[-1]
    span = turned_s.shape[-2]
    core, clip = lax.axis_index("seq") % 2, lax.axis_index("dp")
    for at, ref in enumerate(sources):
        turned = jnp.transpose(ref[...].astype(F32))
        for b in range(blocks * 2 * clips):
            rows = turned[b * span : (b + 1) * span]
            turned_s[at, b // (2 * clips), b % (2 * clips)] = rows.astype(BF)
        for u in range(2):
            for w in range(clips):
                own = (core ^ u) * clips + (clip ^ w)
                for b in range(blocks):
                    pieces[u * clips + w][at, b] = turned_s[at, b, own]


def attention_kernel(heads, sharers, rows, block, factor, *refs):
    key_group_ref, query_group_ref = refs[:2]
    at = 2
    own = refs[at : at + heads]
    at += heads
    shared = refs[at : at + heads * (sharers - 1)]
    at += heads * (sharers - 1)
    ups = refs[at : at + heads]
    at += heads
    outs = refs[at : at + heads]
    at += heads
    key_grads = refs[at : at + sharers]
    at += sharers
    key_s, value_s, query_s, up_s, out_s, dk_s, dv_s, sems = refs[at:]
    head, part = head_place(heads)
    dim = key_s.shape[-1]
    span = heads * sharers * rows
    total = heads * rows
    copies = Copies(sems)
    for t in range(heads):
        m = head ^ t
        for u in range(1, sharers):
            piece = shared[t * (sharers - 1) + u - 1]
            copies.start(piece.at[1], key_s.at[m * sharers + (part ^ u)])
            copies.start(piece.at[2], value_s.at[m * sharers + (part ^ u)])
        if t:
            copies.start(own[t].at[0], query_s.at[m])
            copies.start(own[t].at[1], key_s.at[m * sharers + part])
            copies.start(own[t].at[2], value_s.at[m * sharers + part])
            copies.start(ups[t], up_s.at[m])
    query_s[head] = own[0][0]
    key_s[head * sharers + part] = own[0][1]
    value_s[head * sharers + part] = own[0][2]
    up_s[head] = ups[0][...]
    dk_s[...] = jnp.zeros_like(dk_s)
    dv_s[...] = jnp.zeros_like(dv_s)
    group_col = jnp.transpose(jnp.broadcast_to(key_group_ref[...], (128, span)))
    group_col = jnp.concatenate([group_col] * (-(-block // 128)), axis=1)[:, :block]
    copies.wait()
    keys = key_s[...].reshape(span, dim)
    values = value_s[...].reshape(span, dim)
    queries = query_s[...].reshape(total, dim)
    upstream = up_s[...].reshape(total, dim)
    scale = factor * math.log2(math.e)
    for j in range(total // block):
        last = ((j + 1) * block - 1) // rows
        reach = min(span, round_up((last + 1) * sharers * rows + GROUP_MOST - 1, 128))
        lanes = slice(j * block, (j + 1) * block)
        query = queries[lanes]
        up = upstream[lanes]
        key = keys[:reach]
        value = values[:reach]
        logits = lax.dot_general(key, query, OVER_LAST, preferred_element_type=F32)
        logits = jnp.where(group_col[:reach] <= query_group_ref[:, lanes], logits, NEG_FILL)
        row_max = jnp.max(logits, axis=0, keepdims=True)
        unnorm = jnp.exp2((logits - row_max) * scale)
        inverse = 1.0 / jnp.sum(unnorm, axis=0, keepdims=True)
        out = lax.dot_general(value, unnorm.astype(BF), OVER_FIRST, preferred_element_type=F32)
        out = (out * inverse).astype(BF)
        up_t = jnp.transpose(up.astype(F32))
        out_dot = jnp.sum(up_t * out.astype(F32), axis=0, keepdims=True)
        probs = unnorm * inverse
        grad_probs = lax.dot_general(value, up, OVER_LAST, preferred_element_type=F32)
        grad_logits = (probs * (grad_probs - out_dot)).astype(BF)
        grad_query = lax.dot_general(key, grad_logits, OVER_FIRST, preferred_element_type=F32)
        out_s[0, lanes, :] = jnp.transpose(out.astype(F32)).astype(BF)
        out_s[1, lanes, :] = jnp.transpose(grad_query * factor).astype(BF)
        dk_s[:reach, :] += jnp.dot(grad_logits, query, preferred_element_type=F32)
        dv_s[:reach, :] += jnp.dot(probs.astype(BF), up, preferred_element_type=F32)
    for t in range(heads):
        m = head ^ t
        for u in range(sharers):
            there = pl.ds(pl.multiple_of((m * sharers + (part ^ u)) * rows, 64), rows)
            ref = key_grads[u]
            ref[t, 0] = (dk_s[there, :] * factor).astype(ref.dtype)
            ref[t, 1] = dv_s[there, :].astype(ref.dtype)
        here = pl.ds(pl.multiple_of(m * rows, 64), rows)
        outs[t][...] = out_s[:, here, :]


def attention_groups(part, group_ids, clip_length, heads, sharers):
    span = group_ids.shape[0]
    positions = lax.iota(jnp.int32, span)
    key_group = jnp.where(positions < clip_length, group_ids, NO_GROUP)[None, :]
    query_group = lax.dynamic_index_in_dim(
        group_ids.reshape(heads, sharers, span // (heads * sharers)), part, 1, keepdims=False
    ).reshape(1, span // sharers)
    return key_group, query_group


def attention(key_group, query_group, own, shared, ups, after):
    heads = len(own)
    sharers = len(shared) // heads + 1
    rows, width = ups[0].shape
    span = heads * sharers * rows
    total = heads * rows
    block = 256 if total % 256 == 0 else total
    pair = (2, rows, width)
    got = call(
        functools.partial(attention_kernel, heads, sharers, rows, block, width ** (-0.5)),
        "attention",
        [(pair, BF)] * heads + [((heads,) + pair, F32)] + [((heads,) + pair, BF)] * (sharers - 1),
        [key_group, query_group, *own, *shared, *ups],
        [
            ((heads * sharers, rows, width), BF),
            ((heads * sharers, rows, width), BF),
            ((heads, rows, width), BF),
            ((heads, rows, width), BF),
            ((2, total, width), BF),
            ((span, width), F32),
            ((span, width), F32),
        ],
        ATTENTION_MIB,
        12 * total * span * width,
        after,
        [VMEM] * 3
        + [HBM] * (heads - 1 + heads * (sharers - 1))
        + [VMEM]
        + [HBM] * (heads - 1),
        2 * heads * (sharers - 1) + 4 * (heads - 1),
    )
    return got[:heads], got[heads:]


def share_kernel(sharers, *refs):
    terms, sums = refs[:sharers], refs[sharers:]
    for t, ref in enumerate(sums):
        total = terms[0][t]
        for u in range(1, sharers):
            total = total + terms[u][t].astype(F32)
        ref[...] = total.astype(BF)


def query_kernel(heads, *refs):
    gain_ref, raw_ref = refs[:2]
    pieces, (rows_ref, grad_ref) = refs[2 : 2 + heads], refs[2 + heads :]
    inner = raw_ref.shape[-1]
    dim = inner // heads
    head, _ = head_place(heads)
    for t in range(heads):
        own = head ^ t
        rows_ref[:, columns_of(own, dim)] = pieces[t][0]
        grad = norm_back(
            raw_ref[0, :, columns_of(own, dim)],
            gain_ref[pl.ds(own, 1), :],
            pieces[t][1].astype(F32),
        )
        grad_ref[:, columns_of(own, dim)] = grad.astype(BF)


def key_kernel(heads, *refs):
    gain_ref, raw_ref = refs[:2]
    pieces, (key_ref, value_ref) = refs[2 : 2 + heads], refs[2 + heads :]
    inner = raw_ref.shape[-1]
    dim = inner // heads
    head, _ = head_place(heads)
    for t in range(heads):
        own = head ^ t
        grad = norm_back(
            raw_ref[1, :, columns_of(own, dim)],
            gain_ref[pl.ds(own, 1), :],
            pieces[t][0].astype(F32),
        )
        key_ref[:, columns_of(own, dim)] = grad.astype(BF)
        value_ref[:, columns_of(own, dim)] = pieces[t][1]


def mix_kernel(rows_ref, weight_ref, *refs):
    whole_s = refs[-1]
    whole_s[...] = jnp.dot(rows_ref[...], weight_ref[...], preferred_element_type=F32)
    write_width(whole_s, refs[:-1])


def hidden_kernel(width_count, *refs):
    grads, (weight_ref, mod_ref, inv_ref) = refs[:3], refs[3:6]
    inputs = refs[6 : 6 + width_count]
    dot_ref = refs[6 + width_count]
    outs = refs[7 + width_count : -2]
    whole_s, inputs_s = refs[-2:]
    spread(inputs, inputs_s)
    total = 0.0
    for at, grad in enumerate(grads):
        total = total + lax.dot_general(
            grad[...], weight_ref[at], OVER_LAST, preferred_element_type=F32
        )
    whole_s[...] = total
    write_width(whole_s, outs)
    model_width = inputs_s.shape[1]
    scale = 1.0 + mod_ref[:, :model_width].astype(F32)
    normed = inputs_s[...].astype(F32) * inv_ref[...]
    dot = jnp.sum(whole_s[...] * scale * normed, axis=1, keepdims=True)
    turned = jnp.transpose(jnp.broadcast_to(dot, (dot.shape[0], LANES)))
    dot_ref[...] = turned[:8]


def halve(total, step, send_ref, keep_ref):
    odd = (lax.axis_index("seq") // step) % 2 == 1
    for b in range(total.shape[0] // 2):
        first, second = total[2 * b], total[2 * b + 1]
        keep_ref[b] = jnp.where(odd, second, first)
        send_ref[b] = jnp.where(odd, first, second).astype(BF)


def outer_kernel(which, *refs):
    count = (len(refs) - 2) // 2
    lefts, rights = refs[:count], refs[count : 2 * count]
    _, blocks, span, rows = lefts[0].shape
    total = 0.0
    for left, right in zip(lefts, rights):
        total = total + jnp.dot(
            left[which].reshape(blocks * span, rows), right[...], preferred_element_type=F32
        )
    halve(total.reshape(blocks, span, total.shape[1]), 2, *refs[2 * count :])


def step_kernel(step, got_ref, kept_ref, send_ref, keep_ref):
    halve(kept_ref[...] + got_ref[...].astype(F32), step, send_ref, keep_ref)


def halves(blocks, span, width):
    return [((blocks // 2, span, width), BF), ((blocks // 2, span, width), F32)]


class WeightSum:
    def __init__(self, lefts, which, right):
        rights = [right] + [swap(right, "dp", w) for w in range(1, lax.axis_size("dp"))]
        self.rights = rights + [swap(far, "seq", 1) for far in rights]
        self.lefts, self.which, self.step = lefts, which, 2

    def outer(self, after):
        _, blocks, span, rows = self.lefts[0].shape
        width = self.rights[0].shape[1]
        self.send, self.keep = call(
            functools.partial(outer_kernel, self.which),
            "weight_sum",
            halves(blocks, span, width),
            [*self.lefts, *self.rights],
            [],
            8,
            2 * blocks * span * rows * width * len(self.lefts),
            after,
        )
        return [self.send]

    def exchange(self):
        self.got = swap(self.send, "seq", self.step)
        self.step *= 2

    def halve(self, after):
        self.send, self.keep = call(
            functools.partial(step_kernel, self.step),
            "weight_step",
            halves(*self.keep.shape),
            [self.got, self.keep],
            [],
            4,
            1 << 22,
            after,
        )
        return [self.send]


def total_kernel(*refs):
    out_ref, in_ref = refs[-1], refs[-2]
    targets = (out_ref, in_ref.at[0], in_ref.at[1], in_ref.at[2])
    for at, target in enumerate(targets):
        target[...] = refs[2 * at][0].astype(F32) + refs[2 * at + 1][0]


def on_device(
    latents, grad_out, sync_mod, w_qkv, w_out, q_gain, k_gain, frame_of, group_id, clip_len
):
    latents, grad_out, sync_mod = latents[0], grad_out[0], sync_mod[0]
    frame_of, group_id, clip_len = frame_of[0], group_id[0], clip_len[0]
    rows, width_part = latents.shape
    frame_count = sync_mod.shape[0]
    model_width = sync_mod.shape[1] // 2
    heads, head_dim = q_gain.shape
    inner = heads * head_dim
    count, clips = lax.axis_size("seq"), lax.axis_size("dp")
    sharers = count // heads
    seq = lax.axis_index("seq")
    _, part = head_place(heads)
    model_place = lax.axis_index("mp")

    inputs = width_pieces(latents)
    upstream = width_pieces(grad_out)
    width_count = len(inputs)

    back = max(frame_count * j - (FRAME_UP * rows * j) // FRAME_DOWN for j in range(count))
    back = min(frame_count, round_up(max(back, 1), 16))
    earlier = lax.ppermute(
        sync_mod[frame_count - back :], "seq", [(i, i + 1) for i in range(count - 1)]
    )
    window = jnp.concatenate([earlier, sync_mod], axis=0)
    local_frame = frame_of - (seq * frame_count - back)
    selector = (
        local_frame[:, None] == lax.iota(jnp.int32, frame_count + back)[None, :]
    ).astype(BF)
    mod = jnp.dot(selector, window, preferred_element_type=F32).astype(BF)

    key_group, query_group = attention_groups(part, group_id, clip_len, heads, sharers)
    weight = jnp.transpose(w_qkv, (1, 0, 2))
    staged = [weight, w_out, key_group, query_group]
    weight, w_out, key_group, query_group = call(
        functools.partial(stage_kernel, len(staged)),
        "stage",
        [(array.shape, array.dtype) for array in staged],
        staged,
        [],
        2,
        1 << 22,
        [mod],
        [HBM, HBM, VMEM, VMEM],
        len(staged),
    )
    got = call(
        functools.partial(project_kernel, heads, width_count),
        "project",
        [((3, rows, head_dim), BF)] * heads
        + [((rows, model_width), BF), ((2, rows, inner), F32), ((rows, 1), F32)],
        [q_gain, k_gain, weight, mod, *inputs],
        [((rows, model_width), BF), ((rows, inner), BF)],
        8,
        6 * rows * model_width * inner,
    )
    own, (hidden, raw, inv_norm) = got[:heads], got[heads:]
    own = [own[0]] + [swap(own[t], "seq", t * sharers) for t in range(1, heads)]
    shared = [swap(own[t], "seq", u) for t in range(heads) for u in range(1, sharers)]

    got = call(
        functools.partial(upstream_kernel, heads, width_count),
        "upstream",
        [((rows, head_dim), BF)] * heads + [((rows, model_width), BF)],
        [w_out, mod, *upstream],
        [((rows, model_width), BF), ((rows, inner), BF)],
        8,
        2 * rows * model_width * inner,
    )
    ups, grad_attn = got[:heads], got[heads]
    ups = [ups[0]] + [swap(ups[t], "seq", t * sharers) for t in range(1, heads)]

    blocks = count // 2
    span = model_width // (count * clips)
    lefts = call(
        functools.partial(turn_kernel, blocks, clips),
        "turn",
        [((2, blocks, span, rows), BF)] * (2 * clips),
        [hidden, grad_attn],
        [((2, blocks, 2 * clips, span, rows), BF)],
        8,
        1 << 28,
    )
    for u in range(2):
        for w in range(clips):
            if u or w:
                pairs = [
                    (s * clips + x, (s ^ u) * clips + (x ^ w))
                    for s in range(count)
                    for x in range(clips)
                ]
                lefts[u * clips + w] = lax.ppermute(lefts[u * clips + w], ("seq", "dp"), pairs)

    outs, key_grads = attention(key_group, query_group, own, shared, ups, lefts[:1])
    back_out = [outs[0]] + [swap(outs[t], "seq", t * sharers) for t in range(1, heads)]
    terms = key_grads[:1] + [swap(key_grads[u], "seq", u) for u in range(1, sharers)]
    pair = (2, rows, head_dim)
    sums = call(
        functools.partial(share_kernel, sharers),
        "share",
        [(pair, BF)] * heads,
        terms,
        [],
        4,
        1 << 24,
    )
    back_key = [sums[0]] + [swap(sums[t], "seq", t * sharers) for t in range(1, heads)]
    out_rows, grad_query = call(
        functools.partial(query_kernel, heads),
        "query_back",
        [((rows, inner), BF)] * 2,
        [q_gain, raw, *back_out],
        [],
        4,
        1 << 24,
        sums[:1],
    )
    sum_out = WeightSum(lefts, 1, out_rows)
    sum_query = WeightSum(lefts, 0, grad_query)
    parts = call(
        mix_kernel,
        "mix",
        width_outs(rows, model_width, width_part),
        [out_rows, w_out],
        [((rows, model_width), F32)],
        8,
        2 * rows * model_width * inner,
    )
    grad_key, grad_value = call(
        functools.partial(key_kernel, heads),
        "key_back",
        [((rows, inner), BF)] * 2,
        [k_gain, raw, *back_key],
        [],
        4,
        1 << 24,
        parts[:1],
    )
    sum_key = WeightSum(lefts, 0, grad_key)
    sum_value = WeightSum(lefts, 0, grad_value)
    token = sum_out.outer([grad_key])
    got = call(
        functools.partial(hidden_kernel, width_count),
        "hidden_back",
        [((8, rows), F32)] + width_outs(rows, model_width, width_part),
        [grad_query, grad_key, grad_value, weight, mod, inv_norm, *inputs],
        [((rows, model_width), F32), ((rows, model_width), BF)],
        8,
        6 * rows * model_width * inner,
        token,
    )
    part_dot, hidden_parts = got[0], got[1:]
    sum_out.exchange()
    token = sum_query.outer([part_dot])
    sum_query.exchange()
    token = sum_key.outer(token)
    sum_key.exchange()
    sums = [sum_out, sum_query, sum_key, sum_value]
    while sum_out.keep.shape[0] > 1:
        for at, total in enumerate(sums):
            token = total.halve(token)
            total.exchange()
            if at == 0 and sum_value.step == 2:
                token = sum_value.outer(token)
                sum_value.exchange()
    pieces = []
    for total in sums:
        pieces.extend([total.got, total.keep])
    grad_wqkv, grad_wout = call(
        total_kernel,
        "weight_total",
        [((3, span, inner), F32), ((span, inner), F32)],
        pieces,
        [],
        4,
        1 << 22,
    )

    attn_mine = width_sum(parts, width_part)
    gate_mine = lax.dynamic_slice_in_dim(
        mod, model_width + model_place * width_part, width_part, 1
    )
    mixed = (latents.astype(F32) + gate_mine.astype(F32) * attn_mine).astype(BF)

    full_dot = part_dot
    for t in range(1, lax.axis_size("mp")):
        full_dot = full_dot + swap(part_dot, "mp", t)
    grad_mine = width_sum(hidden_parts, width_part)
    scale_mine = lax.dynamic_slice_in_dim(mod, model_place * width_part, width_part, 1)
    normed_mine = latents.astype(F32) * inv_norm
    grad_normed = grad_mine * (1.0 + scale_mine.astype(F32))
    inner_mean = full_dot[0][:, None] / model_width
    grad_inputs = inv_norm * (grad_normed - normed_mine * inner_mean)
    grad_latents = (grad_out.astype(F32) + grad_inputs).astype(BF)

    return (
        mixed[None],
        grad_latents[None],
        jnp.transpose(grad_wqkv, (1, 0, 2)),
        jnp.transpose(grad_wout),
    )


def solution(mesh):
    in_specs = (
        P("dp", "seq", "mp"),
        P("dp", "seq", "mp"),
        P("dp", "seq", None),
        P(None, None, "mp"),
        P("mp", None),
        P("mp", None),
        P("mp", None),
        P("dp", "seq"),
        P("dp", None),
        P("dp"),
    )
    out_specs = (
        P("dp", "seq", "mp"),
        P("dp", "seq", "mp"),
        P(("seq", "dp"), None, "mp"),
        P("mp", ("seq", "dp")),
    )
    return jax.shard_map(
        on_device, mesh=mesh, in_specs=in_specs, out_specs=out_specs, check_vma=False
    )
```

```python
import functools
import math

import jax
import jax.numpy as jnp
from jax import lax
from jax.experimental import pallas as pl
from jax.experimental.pallas import tpu as pltpu
from jax.sharding import PartitionSpec as P

EPSILON = 1e-06
NEG_FILL = -1e30
GROUP_MOST = 96
FRAME_UP, FRAME_DOWN = 96, 125
NO_GROUP = 1 << 30
ATTENTION_MIB = 16
COST = {}
ORDER = ("share", "query", "mix", "key", "a", "a", "hidden", "b", "b", "a", "b", "mixed", "latents")
SPLIT = False
LEFT_FIRST = True
LIMITS = {"share": 1, "query_back": 1, "key_back": 1, "weight_total": 1}
LANES = 128
BF = jnp.bfloat16
F32 = jnp.float32
ANY = pl.BlockSpec(memory_space=pl.ANY)
HBM = pl.BlockSpec(memory_space=pltpu.HBM)
VMEM = pl.BlockSpec(memory_space=pltpu.VMEM)
OVER_LAST = (((1,), (1,)), ((), ()))
OVER_FIRST = (((0,), (0,)), ((), ()))


def swap(value, axis, distance):
    count = lax.axis_size(axis)
    return lax.ppermute(value, axis, [(i, i ^ distance) for i in range(count)])


def unxor(pieces, place):
    pieces = list(pieces)
    for bit in range((len(pieces) - 1).bit_length()):
        odd = ((place >> bit) & 1) == 1
        pieces = [jnp.where(odd, pieces[j ^ (1 << bit)], pieces[j]) for j in range(len(pieces))]
    return pieces


def inv_rms(values):
    return lax.rsqrt(jnp.mean(values * values, axis=-1, keepdims=True) + EPSILON)


def norm_back(raw, gains, upstream):
    inv_norm = inv_rms(raw)
    inner_dot = jnp.mean(upstream * gains * raw, axis=-1, keepdims=True)
    return inv_norm * (gains * upstream - raw * inv_norm * inv_norm * inner_dot)


def round_up(value, step):
    return -(-value // step) * step


def head_place(heads):
    sharers = lax.axis_size("seq") // heads
    seq = lax.axis_index("seq")
    return seq // sharers, seq % sharers


def call(kernel, name, out, args, scratch, mib, flops, after=(), specs=None, copies=0):
    mib = LIMITS.get(name, mib)
    given, late = len(args), len(after)

    def body(*refs):
        kernel(*refs[:given], *refs[given + late :])

    scratch = [pltpu.VMEM(*s) for s in scratch]
    if copies:
        scratch.append(pltpu.SemaphoreType.DMA((copies,)))
    return list(
        pl.pallas_call(
            body,
            out_shape=[jax.ShapeDtypeStruct(*o) for o in out],
            in_specs=(specs or [VMEM] * given) + [ANY] * late,
            out_specs=[VMEM] * len(out),
            scratch_shapes=scratch,
            compiler_params=pltpu.CompilerParams(vmem_limit_bytes=int(mib * (1 << 20))),
            cost_estimate=pl.CostEstimate(
                flops=0, bytes_accessed=COST.get(name, 1) << 10, transcendentals=0
            ),
            name=name,
        )(*args, *after)
    )


class Copies:
    def __init__(self, sems):
        self.sems, self.made = sems, []

    def start(self, source, target):
        copy = pltpu.make_async_copy(source, target, self.sems.at[len(self.made)])
        copy.start()
        self.made.append(copy)

    def wait(self):
        for copy in self.made:
            copy.wait()


def stage_kernel(count, *refs):
    copies = Copies(refs[-1])
    for source, target in zip(refs[:count], refs[count : 2 * count]):
        copies.start(source, target)
    copies.wait()


def columns_of(place, width):
    return pl.ds(pl.multiple_of(place * width, LANES), width)


def spread(pieces, target):
    place = lax.axis_index("mp")
    width = pieces[0].shape[-1]
    for t, piece in enumerate(pieces):
        if len(pieces) == 1:
            target[...] = piece[...]
        else:
            target[:, columns_of(place ^ t, width)] = piece[...]


def width_pieces(value):
    pieces = [value] + [swap(value, "mp", t) for t in range(1, lax.axis_size("mp"))]
    if value.shape[-1] % LANES:
        return [jnp.concatenate(unxor(pieces, lax.axis_index("mp")), axis=-1)]
    return pieces


def width_outs(rows, width, width_part, extra=0):
    if width_part % LANES:
        return [((rows, width), F32)]
    others = width // width_part - 1
    return [((rows, width_part), F32)] + [((rows, width_part + extra), BF)] * others


def write_width(source, refs):
    if len(refs) == 1:
        refs[0][...] = source[...]
        return
    place = lax.axis_index("mp")
    width = refs[0].shape[-1]
    for t, ref in enumerate(refs):
        ref[:, :width] = source[:, columns_of(place ^ t, width)].astype(ref.dtype)


def width_sum(parts, width_part):
    place = lax.axis_index("mp")
    count = lax.axis_size("mp")
    if width_part % LANES:
        whole = parts[0]
        parts = [
            lax.dynamic_slice_in_dim(whole, (place ^ t) * width_part, width_part, 1)
            for t in range(count)
        ]
    total, beside = parts[0], []
    for t in range(1, count):
        got = swap(parts[t].astype(BF), "mp", t)
        total = total + got[:, :width_part].astype(F32)
        beside.append(got[:, width_part : width_part + 3])
    return total, beside


def project_kernel(heads, width_count, *refs):
    q_gain_ref, k_gain_ref, weight_ref, mod_ref = refs[:4]
    inputs = refs[4 : 4 + width_count]
    refs = refs[4 + width_count :]
    pieces = refs[:heads]
    hidden_ref, raw_ref, inv_ref, inputs_s, values_s = refs[heads:]
    spread(inputs, inputs_s)
    model_width = inputs_s.shape[1]
    values = inputs_s[...].astype(F32)
    inv_norm = inv_rms(values)
    inv_ref[...] = inv_norm
    scale = 1.0 + mod_ref[:, :model_width].astype(F32)
    hidden = (values * inv_norm * scale).astype(BF)
    hidden_ref[...] = hidden
    for at in range(2):
        raw_ref[at] = jnp.dot(hidden, weight_ref[at], preferred_element_type=F32)
    values_s[...] = jnp.dot(hidden, weight_ref[2], preferred_element_type=F32).astype(BF)
    dim = values_s.shape[1] // heads
    head, _ = head_place(heads)
    for t in range(heads):
        own = head ^ t
        columns = columns_of(own, dim)
        for at, gain_ref in enumerate((q_gain_ref, k_gain_ref)):
            raw = raw_ref[at, :, columns]
            pieces[t][at] = (raw * inv_rms(raw) * gain_ref[pl.ds(own, 1), :]).astype(BF)
        pieces[t][2] = values_s[:, columns]


def upstream_kernel(heads, width_count, *refs):
    weight_ref, mod_ref = refs[:2]
    upstream = refs[2 : 2 + width_count]
    refs = refs[2 + width_count :]
    pieces = refs[:heads]
    grad_ref, upstream_s, heads_s = refs[heads:]
    spread(upstream, upstream_s)
    model_width = upstream_s.shape[1]
    grad = (upstream_s[...].astype(F32) * mod_ref[:, model_width:].astype(F32)).astype(BF)
    grad_ref[...] = grad
    heads_s[...] = lax.dot_general(
        grad, weight_ref[...], OVER_LAST, preferred_element_type=F32
    ).astype(BF)
    dim = heads_s.shape[1] // heads
    head, _ = head_place(heads)
    for t in range(heads):
        pieces[t][...] = heads_s[:, columns_of(head ^ t, dim)]


def turn_kernel(count, clips, source_ref, *refs):
    pieces, turned_s = refs[:clips], refs[clips]
    span, rows = turned_s.shape[-2], source_ref.shape[0]
    clip = lax.axis_index("dp")
    turned_s[...] = jnp.zeros_like(turned_s)
    turned = jnp.transpose(source_ref[...].astype(F32))
    for b in range(count * clips):
        turned_s[b % clips, b // clips, :, :rows] = turned[b * span : (b + 1) * span].astype(BF)
    for w in range(clips):
        pieces[w][...] = turned_s[clip ^ w]


def turned(source, after):
    count, clips = lax.axis_size("seq"), lax.axis_size("dp")
    rows, width = source.shape
    shape = (count, width // (count * clips), round_up(rows, LANES))
    pieces = call(
        functools.partial(turn_kernel, count, clips),
        "turn",
        [(shape, BF)] * clips,
        [source],
        [((clips,) + shape, BF)],
        6,
        1 << 27,
        after,
    )
    return [pieces[0]] + [swap(pieces[w], "dp", w) for w in range(1, clips)]


def attention_kernel(heads, sharers, rows, block, factor, *refs):
    key_group_ref, query_group_ref = refs[:2]
    at = 2
    own = refs[at : at + heads]
    at += heads
    shared = refs[at : at + heads * (sharers - 1)]
    at += heads * (sharers - 1)
    ups = refs[at : at + heads]
    at += heads
    outs = refs[at : at + heads]
    at += heads
    key_grads = refs[at : at + sharers]
    at += sharers
    key_s, value_s, query_s, up_s, out_s, dk_s, dv_s, sems = refs[at:]
    head, part = head_place(heads)
    dim = key_s.shape[-1]
    span = heads * sharers * rows
    total = heads * rows
    copies = Copies(sems)
    for t in range(heads):
        m = head ^ t
        for u in range(1, sharers):
            piece = shared[t * (sharers - 1) + u - 1]
            copies.start(piece.at[1], key_s.at[m * sharers + (part ^ u)])
            copies.start(piece.at[2], value_s.at[m * sharers + (part ^ u)])
        if t:
            copies.start(own[t].at[0], query_s.at[m])
            copies.start(own[t].at[1], key_s.at[m * sharers + part])
            copies.start(own[t].at[2], value_s.at[m * sharers + part])
            copies.start(ups[t], up_s.at[m])
    query_s[head] = own[0][0]
    key_s[head * sharers + part] = own[0][1]
    value_s[head * sharers + part] = own[0][2]
    up_s[head] = ups[0][...]
    dk_s[...] = jnp.zeros_like(dk_s)
    dv_s[...] = jnp.zeros_like(dv_s)
    group_col = jnp.transpose(jnp.broadcast_to(key_group_ref[...], (128, span)))
    group_col = jnp.concatenate([group_col] * (-(-block // 128)), axis=1)[:, :block]
    copies.wait()
    keys = key_s[...].reshape(span, dim)
    values = value_s[...].reshape(span, dim)
    queries = query_s[...].reshape(total, dim)
    upstream = up_s[...].reshape(total, dim)
    scale = factor * math.log2(math.e)
    for j in range(total // block):
        last = ((j + 1) * block - 1) // rows
        reach = min(span, round_up((last + 1) * sharers * rows + GROUP_MOST - 1, 128))
        lanes = slice(j * block, (j + 1) * block)
        query = queries[lanes]
        up = upstream[lanes]
        key = keys[:reach]
        value = values[:reach]
        logits = lax.dot_general(key, query, OVER_LAST, preferred_element_type=F32)
        logits = jnp.where(group_col[:reach] <= query_group_ref[:, lanes], logits, NEG_FILL)
        row_max = jnp.max(logits, axis=0, keepdims=True)
        unnorm = jnp.exp2((logits - row_max) * scale)
        inverse = 1.0 / jnp.sum(unnorm, axis=0, keepdims=True)
        out = lax.dot_general(value, unnorm.astype(BF), OVER_FIRST, preferred_element_type=F32)
        out = (out * inverse).astype(BF)
        up_t = jnp.transpose(up.astype(F32))
        out_dot = jnp.sum(up_t * out.astype(F32), axis=0, keepdims=True)
        probs = unnorm * inverse
        grad_probs = lax.dot_general(value, up, OVER_LAST, preferred_element_type=F32)
        grad_logits = (probs * (grad_probs - out_dot)).astype(BF)
        grad_query = lax.dot_general(key, grad_logits, OVER_FIRST, preferred_element_type=F32)
        out_s[0, lanes, :] = jnp.transpose(out.astype(F32)).astype(BF)
        out_s[1, lanes, :] = jnp.transpose(grad_query * factor).astype(BF)
        dk_s[:reach, :] += jnp.dot(grad_logits, query, preferred_element_type=F32)
        dv_s[:reach, :] += jnp.dot(probs.astype(BF), up, preferred_element_type=F32)
    for t in range(heads):
        m = head ^ t
        for u in range(sharers):
            there = pl.ds(pl.multiple_of((m * sharers + (part ^ u)) * rows, 64), rows)
            ref = key_grads[u]
            ref[t, 0] = (dk_s[there, :] * factor).astype(ref.dtype)
            ref[t, 1] = dv_s[there, :].astype(ref.dtype)
        here = pl.ds(pl.multiple_of(m * rows, 64), rows)
        outs[t][...] = out_s[:, here, :]


def attention_groups(part, group_ids, clip_length, heads, sharers):
    span = group_ids.shape[0]
    positions = lax.iota(jnp.int32, span)
    key_group = jnp.where(positions < clip_length, group_ids, NO_GROUP)[None, :]
    query_group = lax.dynamic_index_in_dim(
        group_ids.reshape(heads, sharers, span // (heads * sharers)), part, 1, keepdims=False
    ).reshape(1, span // sharers)
    return key_group, query_group


def attention(key_group, query_group, own, shared, ups, after):
    heads = len(own)
    sharers = len(shared) // heads + 1
    rows, width = ups[0].shape
    span = heads * sharers * rows
    total = heads * rows
    block = 256 if total % 256 == 0 else total
    pair = (2, rows, width)
    got = call(
        functools.partial(attention_kernel, heads, sharers, rows, block, width ** (-0.5)),
        "attention",
        [(pair, BF)] * heads + [((heads,) + pair, F32)] + [((heads,) + pair, BF)] * (sharers - 1),
        [key_group, query_group, *own, *shared, *ups],
        [
            ((heads * sharers, rows, width), BF),
            ((heads * sharers, rows, width), BF),
            ((heads, rows, width), BF),
            ((heads, rows, width), BF),
            ((2, total, width), BF),
            ((span, width), F32),
            ((span, width), F32),
        ],
        ATTENTION_MIB,
        12 * total * span * width,
        after,
        [VMEM] * 3
        + [HBM] * (heads - 1 + heads * (sharers - 1))
        + [VMEM]
        + [HBM] * (heads - 1),
        2 * heads * (sharers - 1) + 4 * (heads - 1),
    )
    return got[:heads], got[heads:]


def share_kernel(sharers, *refs):
    terms, sums = refs[:sharers], refs[sharers:]
    for t, ref in enumerate(sums):
        total = terms[0][t]
        for u in range(1, sharers):
            total = total + terms[u][t].astype(F32)
        ref[...] = total.astype(BF)


def query_kernel(heads, *refs):
    gain_ref, raw_ref = refs[:2]
    pieces, pair_ref = refs[2 : 2 + heads], refs[2 + heads]
    inner = raw_ref.shape[-1]
    dim = inner // heads
    head, _ = head_place(heads)
    for t in range(heads):
        own = head ^ t
        pair_ref[:, columns_of(own, dim)] = pieces[t][0]
        grad = norm_back(
            raw_ref[0, :, columns_of(own, dim)],
            gain_ref[pl.ds(own, 1), :],
            pieces[t][1].astype(F32),
        )
        pair_ref[:, columns_of(heads + own, dim)] = grad.astype(BF)


def key_kernel(heads, *refs):
    gain_ref, raw_ref = refs[:2]
    pieces, pair_ref = refs[2 : 2 + heads], refs[2 + heads]
    inner = raw_ref.shape[-1]
    dim = inner // heads
    head, _ = head_place(heads)
    for t in range(heads):
        own = head ^ t
        grad = norm_back(
            raw_ref[1, :, columns_of(own, dim)],
            gain_ref[pl.ds(own, 1), :],
            pieces[t][0].astype(F32),
        )
        pair_ref[:, columns_of(own, dim)] = grad.astype(BF)
        pair_ref[:, columns_of(heads + own, dim)] = pieces[t][1]


def mix_kernel(rows_ref, weight_ref, *refs):
    whole_s = refs[-1]
    inner = weight_ref.shape[0]
    whole_s[...] = jnp.dot(rows_ref[:, :inner], weight_ref[...], preferred_element_type=F32)
    write_width(whole_s, refs[:-1])


def hidden_kernel(width_count, *refs):
    first_ref, second_ref, weight_ref, mod_ref, inv_ref = refs[:5]
    inputs = refs[5 : 5 + width_count]
    dot_ref = refs[5 + width_count]
    outs = refs[6 + width_count : -4]
    whole_s, inputs_s, weight_s, sems = refs[-4:]
    copies = Copies(sems)
    for at in range(3):
        copies.start(weight_ref.at[at], weight_s.at[at])
    spread(inputs, inputs_s)
    inner = weight_ref.shape[2]
    grads = (first_ref[:, inner:], second_ref[:, :inner], second_ref[:, inner:])
    total = 0.0
    for at, grad in enumerate(grads):
        copies.made[at].wait()
        total = total + lax.dot_general(
            grad, weight_s[at], OVER_LAST, preferred_element_type=F32
        )
    whole_s[...] = total
    write_width(whole_s, outs)
    model_width = inputs_s.shape[1]
    scale = 1.0 + mod_ref[:, :model_width].astype(F32)
    normed = inputs_s[...].astype(F32) * inv_ref[...]
    dot = jnp.sum(whole_s[...] * scale * normed, axis=1, keepdims=True)
    dot_ref[...] = dot
    for ref in outs[1:]:
        high = dot.astype(BF).astype(F32)
        middle = (dot - high).astype(BF).astype(F32)
        low = dot - high - middle
        lane = lax.broadcasted_iota(jnp.int32, (dot.shape[0], LANES), 1)
        beside = jnp.where(lane == 0, high, jnp.where(lane == 1, middle, low))
        ref[:, outs[0].shape[1] :] = beside.astype(BF)


def halve(total, step, send_ref, keep_ref):
    odd = (lax.axis_index("seq") // step) % 2 == 1
    for b in range(total.shape[0] // 2):
        first, second = total[2 * b], total[2 * b + 1]
        keep_ref[b] = jnp.where(odd, second, first)
        send_ref[b] = jnp.where(odd, first, second).astype(BF)


def outer_kernel(clips, *refs):
    rights, (send_ref, keep_ref, total_s) = refs[:clips], refs[-3:]
    lefts = refs[clips:-3]
    blocks, span, lanes = lefts[0].shape
    rows, width = rights[0].shape
    groups = len(lefts) // clips
    width = width // groups
    for at in range(groups):
        columns = slice(at * width, (at + 1) * width)
        total = 0.0
        for left, right in zip(lefts[at * clips : (at + 1) * clips], rights):
            left = left[...].reshape(blocks * span, lanes)[:, :rows]
            total = total + jnp.dot(left, right[:, columns], preferred_element_type=F32)
        total_s[:, :, columns] = total.reshape(blocks, span, width)
    halve(total_s, 1, send_ref, keep_ref)


def step_kernel(step, got_ref, kept_ref, send_ref, keep_ref):
    halve(kept_ref[...] + got_ref[...].astype(F32), step, send_ref, keep_ref)


def halves(blocks, span, width):
    return [((blocks // 2, span, width), BF), ((blocks // 2, span, width), F32)]


class WeightSum:
    def __init__(self, name, lefts, right):
        self.name = name
        far = [swap(right, "dp", w) for w in range(1, lax.axis_size("dp"))]
        self.rights = [right] + far
        self.lefts, self.step = lefts, 1

    def outer(self, after):
        blocks, span, _ = self.lefts[0].shape
        rows, width = self.rights[0].shape
        self.send, self.keep = call(
            functools.partial(outer_kernel, len(self.rights)),
            "weight_sum_" + self.name,
            halves(blocks, span, width),
            [*self.rights, *self.lefts],
            [((blocks, span, width), F32)],
            12,
            2 * blocks * span * rows * width * len(self.rights),
            after,
        )
        return [self.send]

    def exchange(self):
        self.got = swap(self.send, "seq", self.step)
        self.step *= 2

    def halve(self, after):
        self.send, self.keep = call(
            functools.partial(step_kernel, self.step),
            "weight_step_" + self.name,
            halves(*self.keep.shape),
            [self.got, self.keep],
            [],
            4,
            1 << 22,
            after,
        )
        return [self.send]


def total_kernel(*refs):
    in_ref, out_ref = refs[-2:]
    inner = out_ref.shape[1]
    targets = [out_ref, in_ref.at[0], in_ref.at[1], in_ref.at[2]]
    for got, kept in zip(refs[0:-2:2], refs[1:-2:2]):
        for at in range(got.shape[2] // inner):
            columns = slice(at * inner, (at + 1) * inner)
            targets.pop(0)[...] = got[0, :, columns].astype(F32) + kept[0, :, columns]


def finish_mix_kernel(latents_ref, mod_ref, own_ref, *refs):
    gots, out_ref = refs[:-1], refs[-1]
    width = own_ref.shape[1]
    place = lax.axis_index("mp") + mod_ref.shape[1] // 2 // width
    gate = mod_ref[:, columns_of(place, width)].astype(F32)
    total = own_ref[...]
    for got in gots:
        total = total + got[...].astype(F32)
    out_ref[...] = (latents_ref[...].astype(F32) + gate * total).astype(BF)


def finish_latents_kernel(latents_ref, upstream_ref, mod_ref, inv_ref, dot_ref, own_ref, *refs):
    gots, out_ref = refs[:-1], refs[-1]
    width = own_ref.shape[1]
    scale = 1.0 + mod_ref[:, columns_of(lax.axis_index("mp"), width)].astype(F32)
    total, dot = own_ref[...], dot_ref[...]
    for got in gots:
        total = total + got[:, :width].astype(F32)
        lane = lax.broadcasted_iota(jnp.int32, (got.shape[0], LANES), 1)
        beside = jnp.where(lane < 3, got[:, width:].astype(F32), 0.0)
        dot = dot + jnp.sum(beside, axis=1, keepdims=True)
    inv_norm = inv_ref[...]
    normed = latents_ref[...].astype(F32) * inv_norm
    mean = dot * (1.0 / (mod_ref.shape[1] // 2))
    grad = inv_norm * (total * scale - normed * mean)
    out_ref[...] = (upstream_ref[...].astype(F32) + grad).astype(BF)


def finish_mix(latents, mod, parts, after):
    width = latents.shape[1]
    if width % LANES:
        place = lax.axis_index("mp") * width + mod.shape[1] // 2
        gate = lax.dynamic_slice_in_dim(mod, place, width, 1).astype(F32)
        total, _ = width_sum(parts, width)
        return (latents.astype(F32) + gate * total).astype(BF), after
    gots = [swap(parts[t], "mp", t) for t in range(1, len(parts))]
    (mixed,) = call(
        finish_mix_kernel,
        "finish_mix",
        [(latents.shape, BF)],
        [latents, mod, parts[0], *gots],
        [],
        4,
        1 << 22,
        after,
    )
    return mixed, [mixed]


def finish_latents(latents, grad_out, mod, inv_norm, dot, parts, after):
    width = latents.shape[1]
    if width % LANES:
        total, _ = width_sum(parts, width)
        dot = sum([swap(dot, "mp", t) for t in range(1, lax.axis_size("mp"))], dot)
        place = lax.axis_index("mp") * width
        scale = 1.0 + lax.dynamic_slice_in_dim(mod, place, width, 1).astype(F32)
        normed = latents.astype(F32) * inv_norm
        grad = inv_norm * (total * scale - normed * (dot / (mod.shape[1] // 2)))
        return (grad_out.astype(F32) + grad).astype(BF), after
    gots = [swap(parts[t], "mp", t) for t in range(1, len(parts))]
    (grad,) = call(
        finish_latents_kernel,
        "finish_latents",
        [(latents.shape, BF)],
        [latents, grad_out, mod, inv_norm, dot, parts[0], *gots],
        [],
        4,
        1 << 22,
        after,
    )
    return grad, [grad]


def on_device(
    latents, grad_out, sync_mod, w_qkv, w_out, q_gain, k_gain, frame_of, group_id, clip_len
):
    latents, grad_out, sync_mod = latents[0], grad_out[0], sync_mod[0]
    frame_of, group_id, clip_len = frame_of[0], group_id[0], clip_len[0]
    rows, width_part = latents.shape
    frame_count = sync_mod.shape[0]
    model_width = sync_mod.shape[1] // 2
    heads, head_dim = q_gain.shape
    inner = heads * head_dim
    count, clips = lax.axis_size("seq"), lax.axis_size("dp")
    sharers = count // heads
    seq = lax.axis_index("seq")
    _, part = head_place(heads)

    inputs = width_pieces(latents)
    width_count = len(inputs)

    back = max(frame_count * j - (FRAME_UP * rows * j) // FRAME_DOWN for j in range(count))
    back = min(frame_count, round_up(max(back, 1), 16))
    earlier = lax.ppermute(
        sync_mod[frame_count - back :], "seq", [(i, i + 1) for i in range(count - 1)]
    )
    window = jnp.concatenate([earlier, sync_mod], axis=0)
    local_frame = frame_of - (seq * frame_count - back)
    selector = (
        local_frame[:, None] == lax.iota(jnp.int32, frame_count + back)[None, :]
    ).astype(BF)
    mod = jnp.dot(selector, window, preferred_element_type=F32).astype(BF)

    key_group, query_group = attention_groups(part, group_id, clip_len, heads, sharers)
    weight = jnp.transpose(w_qkv, (1, 0, 2))
    weight_far = weight
    staged = [weight, w_out, key_group, query_group, grad_out]
    weight, w_out, key_group, query_group, grad_out = call(
        functools.partial(stage_kernel, len(staged)),
        "stage",
        [(array.shape, array.dtype) for array in staged],
        staged,
        [],
        2,
        1 << 22,
        [mod],
        [HBM, HBM, VMEM, VMEM, HBM],
        len(staged),
    )
    upstream = width_pieces(grad_out)
    got = call(
        functools.partial(project_kernel, heads, width_count),
        "project",
        [((3, rows, head_dim), BF)] * heads
        + [((rows, model_width), BF), ((2, rows, inner), F32), ((rows, 1), F32)],
        [q_gain, k_gain, weight, mod, *inputs],
        [((rows, model_width), BF), ((rows, inner), BF)],
        8,
        6 * rows * model_width * inner,
    )
    own, (hidden, raw, inv_norm) = got[:heads], got[heads:]
    own = [own[0]] + [swap(own[t], "seq", t * sharers) for t in range(1, heads)]
    shared = [swap(own[t], "seq", u) for t in range(heads) for u in range(1, sharers)]

    left_hidden = turned(hidden, [])
    got = call(
        functools.partial(upstream_kernel, heads, width_count),
        "upstream",
        [((rows, head_dim), BF)] * heads + [((rows, model_width), BF)],
        [w_out, mod, *upstream],
        [((rows, model_width), BF), ((rows, inner), BF)],
        8,
        2 * rows * model_width * inner,
        left_hidden[:1],
    )
    ups, grad_attn = got[:heads], got[heads]
    left_grad = turned(grad_attn, [])
    ups = [ups[0]] + [swap(ups[t], "seq", t * sharers) for t in range(1, heads)]

    outs, key_grads = attention(key_group, query_group, own, shared, ups, [*left_hidden[1:], left_grad[0]])
    terms = key_grads[:1] + [swap(key_grads[u], "seq", u) for u in range(1, sharers)]
    pair = (2, rows, head_dim)
    back_out = [outs[0]] + [swap(outs[t], "seq", t * sharers) for t in range(1, heads)]
    state = {}

    def share(after):
        sums = call(
            functools.partial(share_kernel, sharers),
            "share",
            [(pair, BF)] * heads,
            terms,
            [],
            4,
            1 << 24,
            left_grad[1:] if LEFT_FIRST else (),
        )
        state["back_key"] = sums[:1] + [
            swap(sums[t], "seq", t * sharers) for t in range(1, heads)
        ]
        return sums[:1]

    def query(after):
        state["first"] = call(
            functools.partial(query_kernel, heads),
            "query_back",
            [((rows, 2 * inner), BF)],
            [q_gain, raw, *back_out],
            [],
            4,
            1 << 24,
            after,
        )[0]
        state["a"] = WeightSum("a", left_grad + left_hidden, state["first"])
        return [state["first"]]

    def mix(after):
        state["parts"] = call(
            mix_kernel,
            "mix",
            width_outs(rows, model_width, width_part),
            [state["first"], w_out],
            [((rows, model_width), F32)],
            8,
            2 * rows * model_width * inner,
            after,
        )
        return state["parts"][:1]

    def key(after):
        state["second"] = call(
            functools.partial(key_kernel, heads),
            "key_back",
            [((rows, 2 * inner), BF)],
            [k_gain, raw, *state["back_key"]],
            [],
            4,
            1 << 24,
            after,
        )[0]
        if SPLIT:
            state["b"] = WeightSum("b", left_hidden, state["second"][:, :inner])
            state["c"] = WeightSum("c", left_hidden, state["second"][:, inner:])
        else:
            state["b"] = WeightSum("b", left_hidden, state["second"])
        return [state["second"]]

    def advance(name, after):
        total = state[name]
        token = total.halve(after) if hasattr(total, "keep") else total.outer(after)
        total.exchange()
        return token

    def hidden_back(after):
        got = call(
            functools.partial(hidden_kernel, width_count),
            "hidden_back",
            [((rows, 1), F32)] + width_outs(rows, model_width, width_part, LANES),
            [state["first"], state["second"], weight_far, mod, inv_norm, *inputs],
            [
                ((rows, model_width), F32),
                ((rows, model_width), BF),
                (weight_far.shape, BF),
            ],
            10,
            6 * rows * model_width * inner,
            after,
            [VMEM] * 2 + [HBM] + [VMEM] * (2 + width_count),
            3,
        )
        state["dot"], state["hidden"] = got[0], got[1:]
        return [state["dot"]]

    def finish(name, after):
        if name == "mixed":
            state["mixed"], token = finish_mix(latents, mod, state["parts"], after)
        else:
            state["latents"], token = finish_latents(
                latents, grad_out, mod, inv_norm, state["dot"], state["hidden"], after
            )
        return token

    steps = dict(share=share, query=query, mix=mix, key=key, hidden=hidden_back)
    for name in ("a", "b", "c"):
        steps[name] = functools.partial(advance, name)
    for name in ("mixed", "latents"):
        steps[name] = functools.partial(finish, name)
    token = ()
    for name in ORDER:
        token = steps[name](token)
    totals = [state[name] for name in (("a", "b", "c") if SPLIT else ("a", "b"))]
    while totals[-1].keep.shape[0] > 1:
        for total in totals:
            token = total.halve(token)
            total.exchange()
    span = totals[0].keep.shape[1]
    pieces = []
    for total in totals:
        pieces.extend([total.got, total.keep])
    grad_wqkv, grad_wout = call(
        total_kernel,
        "weight_total",
        [((3, span, inner), F32), ((span, inner), F32)],
        pieces,
        [],
        4,
        1 << 22,
    )
    mixed, grad_latents = state["mixed"], state["latents"]
    return (
        mixed[None],
        grad_latents[None],
        jnp.transpose(grad_wqkv, (1, 0, 2)),
        jnp.transpose(grad_wout),
    )


def solution(mesh):
    in_specs = (
        P("dp", "seq", "mp"),
        P("dp", "seq", "mp"),
        P("dp", "seq", None),
        P(None, None, "mp"),
        P("mp", None),
        P("mp", None),
        P("mp", None),
        P("dp", "seq"),
        P("dp", None),
        P("dp"),
    )
    out_specs = (
        P("dp", "seq", "mp"),
        P("dp", "seq", "mp"),
        P(("seq", "dp"), None, "mp"),
        P("mp", ("seq", "dp")),
    )
    return jax.shard_map(
        on_device, mesh=mesh, in_specs=in_specs, out_specs=out_specs, check_vma=False
    )
```

```python
import functools
import math

import jax
import jax.numpy as jnp
from jax import lax
from jax.experimental import pallas as pl
from jax.experimental.pallas import tpu as pltpu
from jax.sharding import PartitionSpec as P

EPSILON = 1e-06
NEG_FILL = -1e30
GROUP_MOST = 96
FRAME_UP, FRAME_DOWN = 96, 125
NO_GROUP = 1 << 30
ATTENTION_MIB = 16
COST = {}
ORDER = ('share', 'query', 'mix', 'key', 'a', 'b', 'a', 'b', 'hidden', 'c', 'd', 'a', 'b', 'c', 'd', 'mixed', 'c', 'd', 'latents')
LEFT_FIRST = True
CORE_PIECES = 2
CLIP_PIECES = {"a": 1, "b": 1, "c": 1, "d": 1}
LIMITS = {"share": 1, "query_back": 1, "key_back": 1, "weight_total": 1}
LANES = 128
BF = jnp.bfloat16
F32 = jnp.float32
ANY = pl.BlockSpec(memory_space=pl.ANY)
HBM = pl.BlockSpec(memory_space=pltpu.HBM)
VMEM = pl.BlockSpec(memory_space=pltpu.VMEM)
OVER_LAST = (((1,), (1,)), ((), ()))
OVER_FIRST = (((0,), (0,)), ((), ()))


def swap(value, axis, distance):
    count = lax.axis_size(axis)
    return lax.ppermute(value, axis, [(i, i ^ distance) for i in range(count)])


def unxor(pieces, place):
    pieces = list(pieces)
    for bit in range((len(pieces) - 1).bit_length()):
        odd = ((place >> bit) & 1) == 1
        pieces = [jnp.where(odd, pieces[j ^ (1 << bit)], pieces[j]) for j in range(len(pieces))]
    return pieces


def inv_rms(values):
    return lax.rsqrt(jnp.mean(values * values, axis=-1, keepdims=True) + EPSILON)


def norm_back(raw, gains, upstream):
    inv_norm = inv_rms(raw)
    inner_dot = jnp.mean(upstream * gains * raw, axis=-1, keepdims=True)
    return inv_norm * (gains * upstream - raw * inv_norm * inv_norm * inner_dot)


def round_up(value, step):
    return -(-value // step) * step


def head_place(heads):
    sharers = lax.axis_size("seq") // heads
    seq = lax.axis_index("seq")
    return seq // sharers, seq % sharers


def call(kernel, name, out, args, scratch, mib, flops, after=(), specs=None, copies=0):
    mib = LIMITS.get(name, mib)
    given, late = len(args), len(after)

    def body(*refs):
        kernel(*refs[:given], *refs[given + late :])

    scratch = [pltpu.VMEM(*s) for s in scratch]
    if copies:
        scratch.append(pltpu.SemaphoreType.DMA((copies,)))
    return list(
        pl.pallas_call(
            body,
            out_shape=[jax.ShapeDtypeStruct(*o) for o in out],
            in_specs=(specs or [VMEM] * given) + [ANY] * late,
            out_specs=[VMEM] * len(out),
            scratch_shapes=scratch,
            compiler_params=pltpu.CompilerParams(vmem_limit_bytes=int(mib * (1 << 20))),
            cost_estimate=pl.CostEstimate(
                flops=0, bytes_accessed=COST.get(name, 1) << 10, transcendentals=0
            ),
            name=name,
        )(*args, *after)
    )


class Copies:
    def __init__(self, sems):
        self.sems, self.made = sems, []

    def start(self, source, target):
        copy = pltpu.make_async_copy(source, target, self.sems.at[len(self.made)])
        copy.start()
        self.made.append(copy)

    def wait(self):
        for copy in self.made:
            copy.wait()


def stage_kernel(count, *refs):
    copies = Copies(refs[-1])
    for source, target in zip(refs[:count], refs[count : 2 * count]):
        copies.start(source, target)
    copies.wait()


def columns_of(place, width):
    return pl.ds(pl.multiple_of(place * width, LANES), width)


def spread(pieces, target):
    place = lax.axis_index("mp")
    width = pieces[0].shape[-1]
    for t, piece in enumerate(pieces):
        if len(pieces) == 1:
            target[...] = piece[...]
        else:
            target[:, columns_of(place ^ t, width)] = piece[...]


def width_pieces(value):
    pieces = [value] + [swap(value, "mp", t) for t in range(1, lax.axis_size("mp"))]
    if value.shape[-1] % LANES:
        return [jnp.concatenate(unxor(pieces, lax.axis_index("mp")), axis=-1)]
    return pieces


def width_outs(rows, width, width_part, extra=0):
    if width_part % LANES:
        return [((rows, width), F32)]
    others = width // width_part - 1
    return [((rows, width_part), F32)] + [((rows, width_part + extra), BF)] * others


def write_width(source, refs):
    if len(refs) == 1:
        refs[0][...] = source[...]
        return
    place = lax.axis_index("mp")
    width = refs[0].shape[-1]
    for t, ref in enumerate(refs):
        ref[:, :width] = source[:, columns_of(place ^ t, width)].astype(ref.dtype)


def width_sum(parts, width_part):
    place = lax.axis_index("mp")
    count = lax.axis_size("mp")
    if width_part % LANES:
        whole = parts[0]
        parts = [
            lax.dynamic_slice_in_dim(whole, (place ^ t) * width_part, width_part, 1)
            for t in range(count)
        ]
    total, beside = parts[0], []
    for t in range(1, count):
        got = swap(parts[t].astype(BF), "mp", t)
        total = total + got[:, :width_part].astype(F32)
        beside.append(got[:, width_part : width_part + 3])
    return total, beside


def project_kernel(heads, width_count, *refs):
    q_gain_ref, k_gain_ref, weight_ref, mod_ref = refs[:4]
    inputs = refs[4 : 4 + width_count]
    refs = refs[4 + width_count :]
    pieces = refs[:heads]
    hidden_ref, raw_ref, inv_ref, inputs_s, values_s = refs[heads:]
    spread(inputs, inputs_s)
    model_width = inputs_s.shape[1]
    values = inputs_s[...].astype(F32)
    inv_norm = inv_rms(values)
    inv_ref[...] = inv_norm
    scale = 1.0 + mod_ref[:, :model_width].astype(F32)
    hidden = (values * inv_norm * scale).astype(BF)
    hidden_ref[...] = hidden
    for at in range(2):
        raw_ref[at] = jnp.dot(hidden, weight_ref[at], preferred_element_type=F32)
    values_s[...] = jnp.dot(hidden, weight_ref[2], preferred_element_type=F32).astype(BF)
    dim = values_s.shape[1] // heads
    head, _ = head_place(heads)
    for t in range(heads):
        own = head ^ t
        columns = columns_of(own, dim)
        for at, gain_ref in enumerate((q_gain_ref, k_gain_ref)):
            raw = raw_ref[at, :, columns]
            pieces[t][at] = (raw * inv_rms(raw) * gain_ref[pl.ds(own, 1), :]).astype(BF)
        pieces[t][2] = values_s[:, columns]


def upstream_kernel(heads, width_count, *refs):
    weight_ref, mod_ref = refs[:2]
    upstream = refs[2 : 2 + width_count]
    refs = refs[2 + width_count :]
    pieces = refs[:heads]
    grad_ref, upstream_s, heads_s = refs[heads:]
    spread(upstream, upstream_s)
    model_width = upstream_s.shape[1]
    grad = (upstream_s[...].astype(F32) * mod_ref[:, model_width:].astype(F32)).astype(BF)
    grad_ref[...] = grad
    heads_s[...] = lax.dot_general(
        grad, weight_ref[...], OVER_LAST, preferred_element_type=F32
    ).astype(BF)
    dim = heads_s.shape[1] // heads
    head, _ = head_place(heads)
    for t in range(heads):
        pieces[t][...] = heads_s[:, columns_of(head ^ t, dim)]


def turn_kernel(count, clips, source_ref, *refs):
    pieces, turned_s = refs[:clips], refs[clips]
    span, rows = turned_s.shape[-2], source_ref.shape[0]
    clip = lax.axis_index("dp")
    turned_s[...] = jnp.zeros_like(turned_s)
    turned = jnp.transpose(source_ref[...].astype(F32))
    for b in range(count * clips):
        turned_s[b % clips, b // clips, :, :rows] = turned[b * span : (b + 1) * span].astype(BF)
    for w in range(clips):
        pieces[w][...] = turned_s[clip ^ w]


def turned(source, after):
    count, clips = lax.axis_size("seq"), lax.axis_size("dp")
    rows, width = source.shape
    shape = (count, width // (count * clips), round_up(rows, LANES))
    pieces = call(
        functools.partial(turn_kernel, count, clips),
        "turn",
        [(shape, BF)] * clips,
        [source],
        [((clips,) + shape, BF)],
        6,
        1 << 27,
        after,
    )
    return [pieces[0]] + [swap(pieces[w], "dp", w) for w in range(1, clips)]


def gather_kernel(heads, *refs):
    out_ref = refs[heads]
    for t in range(heads):
        out_ref[t] = refs[t][1:]


def attention_kernel(heads, sharers, rows, block, factor, *refs):
    key_group_ref, query_group_ref = refs[:2]
    at = 2
    own = refs[at : at + heads]
    at += heads
    shared = refs[at : at + sharers - 1]
    at += sharers - 1
    ups = refs[at : at + heads]
    at += heads
    outs = refs[at : at + heads]
    at += heads
    key_grads = refs[at : at + sharers]
    at += sharers
    key_s, value_s, query_s, up_s, out_s, dk_s, dv_s, sems = refs[at:]
    head, part = head_place(heads)
    dim = key_s.shape[-1]
    span = heads * sharers * rows
    total = heads * rows
    copies = Copies(sems)
    for t in range(heads):
        m = head ^ t
        for u in range(1, sharers):
            piece = shared[u - 1].at[t]
            copies.start(piece.at[0], key_s.at[m * sharers + (part ^ u)])
            copies.start(piece.at[1], value_s.at[m * sharers + (part ^ u)])
        if t:
            copies.start(own[t].at[0], query_s.at[m])
            copies.start(own[t].at[1], key_s.at[m * sharers + part])
            copies.start(own[t].at[2], value_s.at[m * sharers + part])
            copies.start(ups[t], up_s.at[m])
    query_s[head] = own[0][0]
    key_s[head * sharers + part] = own[0][1]
    value_s[head * sharers + part] = own[0][2]
    up_s[head] = ups[0][...]
    dk_s[...] = jnp.zeros_like(dk_s)
    dv_s[...] = jnp.zeros_like(dv_s)
    group_col = jnp.transpose(jnp.broadcast_to(key_group_ref[...], (128, span)))
    group_col = jnp.concatenate([group_col] * (-(-block // 128)), axis=1)[:, :block]
    copies.wait()
    keys = key_s[...].reshape(span, dim)
    values = value_s[...].reshape(span, dim)
    queries = query_s[...].reshape(total, dim)
    upstream = up_s[...].reshape(total, dim)
    scale = factor * math.log2(math.e)
    for j in range(total // block):
        last = ((j + 1) * block - 1) // rows
        reach = min(span, round_up((last + 1) * sharers * rows + GROUP_MOST - 1, 128))
        lanes = slice(j * block, (j + 1) * block)
        query = queries[lanes]
        up = upstream[lanes]
        key = keys[:reach]
        value = values[:reach]
        logits = lax.dot_general(key, query, OVER_LAST, preferred_element_type=F32)
        logits = jnp.where(group_col[:reach] <= query_group_ref[:, lanes], logits, NEG_FILL)
        row_max = jnp.max(logits, axis=0, keepdims=True)
        unnorm = jnp.exp2((logits - row_max) * scale)
        inverse = 1.0 / jnp.sum(unnorm, axis=0, keepdims=True)
        out = lax.dot_general(value, unnorm.astype(BF), OVER_FIRST, preferred_element_type=F32)
        out = (out * inverse).astype(BF)
        up_t = jnp.transpose(up.astype(F32))
        out_dot = jnp.sum(up_t * out.astype(F32), axis=0, keepdims=True)
        probs = unnorm * inverse
        grad_probs = lax.dot_general(value, up, OVER_LAST, preferred_element_type=F32)
        grad_logits = (probs * (grad_probs - out_dot)).astype(BF)
        grad_query = lax.dot_general(key, grad_logits, OVER_FIRST, preferred_element_type=F32)
        out_s[0, lanes, :] = jnp.transpose(out.astype(F32)).astype(BF)
        out_s[1, lanes, :] = jnp.transpose(grad_query * factor).astype(BF)
        dk_s[:reach, :] += jnp.dot(grad_logits, query, preferred_element_type=F32)
        dv_s[:reach, :] += jnp.dot(probs.astype(BF), up, preferred_element_type=F32)
    for t in range(heads):
        m = head ^ t
        for u in range(sharers):
            there = pl.ds(pl.multiple_of((m * sharers + (part ^ u)) * rows, 64), rows)
            ref = key_grads[u]
            ref[t, 0] = (dk_s[there, :] * factor).astype(ref.dtype)
            ref[t, 1] = dv_s[there, :].astype(ref.dtype)
        here = pl.ds(pl.multiple_of(m * rows, 64), rows)
        outs[t][...] = out_s[:, here, :]


def attention_groups(part, group_ids, clip_length, heads, sharers):
    span = group_ids.shape[0]
    positions = lax.iota(jnp.int32, span)
    key_group = jnp.where(positions < clip_length, group_ids, NO_GROUP)[None, :]
    query_group = lax.dynamic_index_in_dim(
        group_ids.reshape(heads, sharers, span // (heads * sharers)), part, 1, keepdims=False
    ).reshape(1, span // sharers)
    return key_group, query_group


def attention(key_group, query_group, own, shared, ups, after):
    heads = len(own)
    sharers = len(shared) + 1
    rows, width = ups[0].shape
    span = heads * sharers * rows
    total = heads * rows
    block = 256 if total % 256 == 0 else total
    pair = (2, rows, width)
    got = call(
        functools.partial(attention_kernel, heads, sharers, rows, block, width ** (-0.5)),
        "attention",
        [(pair, BF)] * heads + [((heads,) + pair, F32)] + [((heads,) + pair, BF)] * (sharers - 1),
        [key_group, query_group, *own, *shared, *ups],
        [
            ((heads * sharers, rows, width), BF),
            ((heads * sharers, rows, width), BF),
            ((heads, rows, width), BF),
            ((heads, rows, width), BF),
            ((2, total, width), BF),
            ((span, width), F32),
            ((span, width), F32),
        ],
        ATTENTION_MIB,
        12 * total * span * width,
        after,
        [VMEM] * 3
        + [HBM] * (heads - 1 + sharers - 1)
        + [VMEM]
        + [HBM] * (heads - 1),
        2 * heads * (sharers - 1) + 4 * (heads - 1),
    )
    return got[:heads], got[heads:]


def share_kernel(sharers, *refs):
    terms, sums = refs[:sharers], refs[sharers:]
    for t, ref in enumerate(sums):
        total = terms[0][t]
        for u in range(1, sharers):
            total = total + terms[u][t].astype(F32)
        ref[...] = total.astype(BF)


def query_kernel(heads, parts, *refs):
    gain_ref, raw_ref = refs[:2]
    pieces, outs = refs[2 : 2 + heads], refs[2 + heads :]
    row_refs, grad_refs = outs[:parts], outs[parts:]
    inner = raw_ref.shape[-1]
    dim = inner // heads
    head, _ = head_place(heads)
    for t in range(heads):
        own = head ^ t
        write_pieces(row_refs, own, pieces[t][0])
        grad = norm_back(
            raw_ref[0, :, columns_of(own, dim)],
            gain_ref[pl.ds(own, 1), :],
            pieces[t][1].astype(F32),
        )
        write_pieces(grad_refs, own, grad.astype(BF))


def key_kernel(heads, parts, *refs):
    gain_ref, raw_ref = refs[:2]
    pieces, outs = refs[2 : 2 + heads], refs[2 + heads :]
    key_refs, value_refs = outs[:parts], outs[parts:]
    inner = raw_ref.shape[-1]
    dim = inner // heads
    head, _ = head_place(heads)
    for t in range(heads):
        own = head ^ t
        grad = norm_back(
            raw_ref[1, :, columns_of(own, dim)],
            gain_ref[pl.ds(own, 1), :],
            pieces[t][0].astype(F32),
        )
        write_pieces(key_refs, own, grad.astype(BF))
        write_pieces(value_refs, own, pieces[t][1])


def join_columns(refs):
    return jnp.concatenate([ref[...] for ref in refs], axis=1)


def mix_kernel(parts, *refs):
    rows, weight_ref, whole_s = refs[:parts], refs[parts], refs[-1]
    whole_s[...] = jnp.dot(join_columns(rows), weight_ref[...], preferred_element_type=F32)
    write_width(whole_s, refs[parts + 1 : -1])


def hidden_kernel(width_count, parts, *refs):
    grads = []
    for part in parts:
        grads.append(join_columns(refs[:part]))
        refs = refs[part:]
    refs = (None,) * 3 + refs
    weight_ref, mod_ref, inv_ref = refs[3:6]
    inputs = refs[6 : 6 + width_count]
    dot_ref = refs[6 + width_count]
    outs = refs[7 + width_count : -4]
    whole_s, inputs_s, weight_s, sems = refs[-4:]
    copies = Copies(sems)
    for at in range(3):
        copies.start(weight_ref.at[at], weight_s.at[at])
    spread(inputs, inputs_s)
    total = 0.0
    for at, grad in enumerate(grads):
        copies.made[at].wait()
        total = total + lax.dot_general(
            grad, weight_s[at], OVER_LAST, preferred_element_type=F32
        )
    whole_s[...] = total
    write_width(whole_s, outs)
    model_width = inputs_s.shape[1]
    scale = 1.0 + mod_ref[:, :model_width].astype(F32)
    normed = inputs_s[...].astype(F32) * inv_ref[...]
    dot = jnp.sum(whole_s[...] * scale * normed, axis=1, keepdims=True)
    dot_ref[...] = dot
    for ref in outs[1:]:
        high = dot.astype(BF).astype(F32)
        middle = (dot - high).astype(BF).astype(F32)
        low = dot - high - middle
        lane = lax.broadcasted_iota(jnp.int32, (dot.shape[0], LANES), 1)
        beside = jnp.where(lane == 0, high, jnp.where(lane == 1, middle, low))
        ref[:, outs[0].shape[1] :] = beside.astype(BF)


def halve(total, step, sends, keep_ref):
    odd = (lax.axis_index("seq") // step) % 2 == 1
    each = sends[0].shape[0]
    for b in range(total.shape[0] // 2):
        first, second = total[2 * b], total[2 * b + 1]
        keep_ref[b] = jnp.where(odd, second, first)
        sends[b // each][b % each] = jnp.where(odd, first, second).astype(BF)


def outer_kernel(clips, pieces, parts, *refs):
    rights, lefts = refs[: clips * pieces], refs[clips * pieces : clips * pieces + clips]
    sends, (keep_ref, total_s) = refs[-2 - parts : -2], refs[-2:]
    blocks, span, lanes = lefts[0].shape
    rows, width = rights[0].shape
    for at in range(pieces):
        total = 0.0
        for w, left in enumerate(lefts):
            left = left[...].reshape(blocks * span, lanes)[:, :rows]
            right = rights[w * pieces + at][...]
            total = total + jnp.dot(left, right, preferred_element_type=F32)
        total_s[:, :, at * width : (at + 1) * width] = total.reshape(blocks, span, width)
    halve(total_s, 1, sends, keep_ref)


def step_kernel(step, parts, *refs):
    gots, (kept_ref, send_ref, keep_ref) = refs[:parts], refs[parts:]
    got = jnp.concatenate([ref[...].astype(F32) for ref in gots], axis=0)
    halve(kept_ref[...] + got, step, [send_ref], keep_ref)


def halves(blocks, span, width, parts=1):
    send = (blocks // 2 // parts, span, width)
    return [(send, BF)] * parts + [((blocks // 2, span, width), F32)]


def clip_pieces(name, width):
    return CLIP_PIECES[name] if width % (CLIP_PIECES[name] * LANES) == 0 else 1


def write_pieces(pieces, place, value):
    width, dim = pieces[0].shape[1], value.shape[1]
    each = width // dim
    for at, piece in enumerate(pieces):
        if len(pieces) == 1:
            piece[:, columns_of(place, dim)] = value
        else:

            @pl.when(place // each == at)
            def _(piece=piece):
                piece[:, columns_of(place % each, dim)] = value


class WeightSum:
    def __init__(self, name, lefts, rights):
        self.name, self.pieces = name, len(rights)
        self.rights = list(rights)
        for w in range(1, lax.axis_size("dp")):
            self.rights.extend(swap(right, "dp", w) for right in rights)
        self.lefts, self.step = lefts, 1

    def outer(self, after):
        blocks, span, _ = self.lefts[0].shape
        rows, width = self.rights[0].shape
        width = width * self.pieces
        parts = min(CORE_PIECES, blocks // 2)
        *self.sends, self.keep = call(
            functools.partial(outer_kernel, len(self.lefts), self.pieces, parts),
            "weight_sum_" + self.name,
            halves(blocks, span, width, parts),
            [*self.rights, *self.lefts],
            [((blocks, span, width), F32)],
            12,
            2 * blocks * span * rows * width * len(self.rights),
            after,
        )
        return [self.sends[0]]

    def exchange(self):
        self.gots = [swap(send, "seq", self.step) for send in self.sends]
        self.step *= 2

    def halve(self, after):
        *self.sends, self.keep = call(
            functools.partial(step_kernel, self.step, len(self.gots)),
            "weight_step_%s%d" % (self.name, self.step),
            halves(*self.keep.shape),
            [*self.gots, self.keep],
            [],
            4,
            1 << 22,
            after,
        )
        return [self.sends[0]]


def total_kernel(*refs):
    in_ref, out_ref = refs[-2:]
    inner = out_ref.shape[1]
    targets = [out_ref, in_ref.at[0], in_ref.at[1], in_ref.at[2]]
    for got, kept in zip(refs[0:-2:2], refs[1:-2:2]):
        for at in range(got.shape[2] // inner):
            columns = slice(at * inner, (at + 1) * inner)
            targets.pop(0)[...] = got[0, :, columns].astype(F32) + kept[0, :, columns]


def finish_mix_kernel(latents_ref, mod_ref, own_ref, *refs):
    gots, out_ref = refs[:-1], refs[-1]
    width = own_ref.shape[1]
    place = lax.axis_index("mp") + mod_ref.shape[1] // 2 // width
    gate = mod_ref[:, columns_of(place, width)].astype(F32)
    total = own_ref[...]
    for got in gots:
        total = total + got[...].astype(F32)
    out_ref[...] = (latents_ref[...].astype(F32) + gate * total).astype(BF)


def finish_latents_kernel(latents_ref, upstream_ref, mod_ref, inv_ref, dot_ref, own_ref, *refs):
    gots, out_ref = refs[:-1], refs[-1]
    width = own_ref.shape[1]
    scale = 1.0 + mod_ref[:, columns_of(lax.axis_index("mp"), width)].astype(F32)
    total, dot = own_ref[...], dot_ref[...]
    for got in gots:
        total = total + got[:, :width].astype(F32)
        lane = lax.broadcasted_iota(jnp.int32, (got.shape[0], LANES), 1)
        beside = jnp.where(lane < 3, got[:, width:].astype(F32), 0.0)
        dot = dot + jnp.sum(beside, axis=1, keepdims=True)
    inv_norm = inv_ref[...]
    normed = latents_ref[...].astype(F32) * inv_norm
    mean = dot * (1.0 / (mod_ref.shape[1] // 2))
    grad = inv_norm * (total * scale - normed * mean)
    out_ref[...] = (upstream_ref[...].astype(F32) + grad).astype(BF)


def finish_mix(latents, mod, parts, after):
    width = latents.shape[1]
    if width % LANES:
        place = lax.axis_index("mp") * width + mod.shape[1] // 2
        gate = lax.dynamic_slice_in_dim(mod, place, width, 1).astype(F32)
        total, _ = width_sum(parts, width)
        return (latents.astype(F32) + gate * total).astype(BF), after
    gots = [swap(parts[t], "mp", t) for t in range(1, len(parts))]
    (mixed,) = call(
        finish_mix_kernel,
        "finish_mix",
        [(latents.shape, BF)],
        [latents, mod, parts[0], *gots],
        [],
        4,
        1 << 22,
        after,
    )
    return mixed, [mixed]


def finish_latents(latents, grad_out, mod, inv_norm, dot, parts, after):
    width = latents.shape[1]
    if width % LANES:
        total, _ = width_sum(parts, width)
        dot = sum([swap(dot, "mp", t) for t in range(1, lax.axis_size("mp"))], dot)
        place = lax.axis_index("mp") * width
        scale = 1.0 + lax.dynamic_slice_in_dim(mod, place, width, 1).astype(F32)
        normed = latents.astype(F32) * inv_norm
        grad = inv_norm * (total * scale - normed * (dot / (mod.shape[1] // 2)))
        return (grad_out.astype(F32) + grad).astype(BF), after
    gots = [swap(parts[t], "mp", t) for t in range(1, len(parts))]
    (grad,) = call(
        finish_latents_kernel,
        "finish_latents",
        [(latents.shape, BF)],
        [latents, grad_out, mod, inv_norm, dot, parts[0], *gots],
        [],
        4,
        1 << 22,
        after,
    )
    return grad, [grad]


def on_device(
    latents, grad_out, sync_mod, w_qkv, w_out, q_gain, k_gain, frame_of, group_id, clip_len
):
    latents, grad_out, sync_mod = latents[0], grad_out[0], sync_mod[0]
    frame_of, group_id, clip_len = frame_of[0], group_id[0], clip_len[0]
    rows, width_part = latents.shape
    frame_count = sync_mod.shape[0]
    model_width = sync_mod.shape[1] // 2
    heads, head_dim = q_gain.shape
    inner = heads * head_dim
    count, clips = lax.axis_size("seq"), lax.axis_size("dp")
    sharers = count // heads
    seq = lax.axis_index("seq")
    _, part = head_place(heads)

    inputs = width_pieces(latents)
    width_count = len(inputs)

    back = max(frame_count * j - (FRAME_UP * rows * j) // FRAME_DOWN for j in range(count))
    back = min(frame_count, round_up(max(back, 1), 16))
    earlier = lax.ppermute(
        sync_mod[frame_count - back :], "seq", [(i, i + 1) for i in range(count - 1)]
    )
    window = jnp.concatenate([earlier, sync_mod], axis=0)
    local_frame = frame_of - (seq * frame_count - back)
    selector = (
        local_frame[:, None] == lax.iota(jnp.int32, frame_count + back)[None, :]
    ).astype(BF)
    mod = jnp.dot(selector, window, preferred_element_type=F32).astype(BF)

    key_group, query_group = attention_groups(part, group_id, clip_len, heads, sharers)
    weight = jnp.transpose(w_qkv, (1, 0, 2))
    weight_far = weight
    staged = [weight, w_out, key_group, query_group, grad_out]
    weight, w_out, key_group, query_group, grad_out = call(
        functools.partial(stage_kernel, len(staged)),
        "stage",
        [(array.shape, array.dtype) for array in staged],
        staged,
        [],
        2,
        1 << 22,
        [mod],
        [HBM, HBM, VMEM, VMEM, HBM],
        len(staged),
    )
    upstream = width_pieces(grad_out)
    got = call(
        functools.partial(project_kernel, heads, width_count),
        "project",
        [((3, rows, head_dim), BF)] * heads
        + [((rows, model_width), BF), ((2, rows, inner), F32), ((rows, 1), F32)],
        [q_gain, k_gain, weight, mod, *inputs],
        [((rows, model_width), BF), ((rows, inner), BF)],
        8,
        6 * rows * model_width * inner,
    )
    own, (hidden, raw, inv_norm) = got[:heads], got[heads:]
    own = [own[0]] + [swap(own[t], "seq", t * sharers) for t in range(1, heads)]
    (keys_values,) = call(
        functools.partial(gather_kernel, heads),
        "gather",
        [((heads, 2, rows, head_dim), BF)],
        own,
        [],
        2,
        0,
    )
    shared = [swap(keys_values, "seq", u) for u in range(1, sharers)]

    left_hidden = turned(hidden, [])
    got = call(
        functools.partial(upstream_kernel, heads, width_count),
        "upstream",
        [((rows, head_dim), BF)] * heads + [((rows, model_width), BF)],
        [w_out, mod, *upstream],
        [((rows, model_width), BF), ((rows, inner), BF)],
        8,
        2 * rows * model_width * inner,
        left_hidden[:1],
    )
    ups, grad_attn = got[:heads], got[heads]
    left_grad = turned(grad_attn, [])
    ups = [ups[0]] + [swap(ups[t], "seq", t * sharers) for t in range(1, heads)]

    outs, key_grads = attention(key_group, query_group, own, shared, ups, [*left_hidden[1:], left_grad[0]])
    terms = key_grads[:1] + [swap(key_grads[u], "seq", u) for u in range(1, sharers)]
    pair = (2, rows, head_dim)
    back_out = [outs[0]] + [swap(outs[t], "seq", t * sharers) for t in range(1, heads)]
    state = {}

    def cut(names, made):
        first = clip_pieces(names[0], inner)
        return made[:first], made[first:]

    def pair_outs(names):
        outs = []
        for name in names:
            pieces = clip_pieces(name, inner)
            outs.extend([((rows, inner // pieces), BF)] * pieces)
        return outs


    def share(after):
        sums = call(
            functools.partial(share_kernel, sharers),
            "share",
            [(pair, BF)] * heads,
            terms,
            [],
            4,
            1 << 24,
            left_grad[1:] if LEFT_FIRST else (),
        )
        state["back_key"] = sums[:1] + [
            swap(sums[t], "seq", t * sharers) for t in range(1, heads)
        ]
        return sums[:1]

    def query(after):
        made = call(
            functools.partial(query_kernel, heads, clip_pieces("a", inner)),
            "query_back",
            pair_outs("ab"),
            [q_gain, raw, *back_out],
            [],
            4,
            1 << 24,
            after,
        )
        state["rows"], state["query"] = cut("ab", made)
        state["a"] = WeightSum("a", left_grad, state["rows"])
        state["b"] = WeightSum("b", left_hidden, state["query"])
        return made[:1]

    def mix(after):
        state["parts"] = call(
            functools.partial(mix_kernel, len(state["rows"])),
            "mix",
            width_outs(rows, model_width, width_part),
            [*state["rows"], w_out],
            [((rows, model_width), F32)],
            8,
            2 * rows * model_width * inner,
            after,
        )
        return state["parts"][:1]

    def key(after):
        made = call(
            functools.partial(key_kernel, heads, clip_pieces("c", inner)),
            "key_back",
            pair_outs("cd"),
            [k_gain, raw, *state["back_key"]],
            [],
            4,
            1 << 24,
            after,
        )
        state["key"], state["value"] = cut("cd", made)
        state["c"] = WeightSum("c", left_hidden, state["key"])
        state["d"] = WeightSum("d", left_hidden, state["value"])
        return made[:1]

    def advance(name, after):
        total = state[name]
        token = total.halve(after) if hasattr(total, "keep") else total.outer(after)
        total.exchange()
        return token

    def hidden_back(after):
        grads = [state[name] for name in ("query", "key", "value")]
        got = call(
            functools.partial(hidden_kernel, width_count, [len(g) for g in grads]),
            "hidden_back",
            [((rows, 1), F32)] + width_outs(rows, model_width, width_part, LANES),
            [*sum(grads, []), weight_far, mod, inv_norm, *inputs],
            [
                ((rows, model_width), F32),
                ((rows, model_width), BF),
                (weight_far.shape, BF),
            ],
            10,
            6 * rows * model_width * inner,
            after,
            [VMEM] * sum(len(g) for g in grads) + [HBM] + [VMEM] * (2 + width_count),
            3,
        )
        state["dot"], state["hidden"] = got[0], got[1:]
        return [state["dot"]]

    def finish(name, after):
        if name == "mixed":
            state["mixed"], token = finish_mix(latents, mod, state["parts"], after)
        else:
            state["latents"], token = finish_latents(
                latents, grad_out, mod, inv_norm, state["dot"], state["hidden"], after
            )
        return token

    steps = dict(share=share, query=query, mix=mix, key=key, hidden=hidden_back)
    for name in "abcd":
        steps[name] = functools.partial(advance, name)
    for name in ("mixed", "latents"):
        steps[name] = functools.partial(finish, name)
    token = ()
    for name in ORDER:
        token = steps[name](token)
    totals = [state[name] for name in "abcd"]
    while max(total.keep.shape[0] for total in totals) > 1:
        for total in totals:
            if total.keep.shape[0] == max(other.keep.shape[0] for other in totals):
                token = total.halve(token)
                total.exchange()
    span = totals[0].keep.shape[1]
    pieces = []
    for total in totals:
        pieces.extend([total.gots[0], total.keep])
    grad_wqkv, grad_wout = call(
        total_kernel,
        "weight_total",
        [((3, span, inner), F32), ((span, inner), F32)],
        pieces,
        [],
        4,
        1 << 22,
    )
    mixed, grad_latents = state["mixed"], state["latents"]
    return (
        mixed[None],
        grad_latents[None],
        jnp.transpose(grad_wqkv, (1, 0, 2)),
        jnp.transpose(grad_wout),
    )


def solution(mesh):
    in_specs = (
        P("dp", "seq", "mp"),
        P("dp", "seq", "mp"),
        P("dp", "seq", None),
        P(None, None, "mp"),
        P("mp", None),
        P("mp", None),
        P("mp", None),
        P("dp", "seq"),
        P("dp", None),
        P("dp"),
    )
    out_specs = (
        P("dp", "seq", "mp"),
        P("dp", "seq", "mp"),
        P(("seq", "dp"), None, "mp"),
        P("mp", ("seq", "dp")),
    )
    return jax.shard_map(
        on_device, mesh=mesh, in_specs=in_specs, out_specs=out_specs, check_vma=False
    )
```

```python
import functools
import math

import jax
import jax.numpy as jnp
from jax import lax
from jax.experimental import pallas as pl
from jax.experimental.pallas import tpu as pltpu
from jax.sharding import PartitionSpec as P

EPSILON = 1e-06
NEG_FILL = -1e30
GROUP_MOST = 96
FRAME_UP, FRAME_DOWN = 96, 125
NO_GROUP = 1 << 30
ATTENTION_MIB = 16
COST = {}
ORDER = ('share', 'query', 'mix', 'key', 'a', 'b', 'a', 'b', 'hidden', 'c', 'd', 'a', 'b', 'c', 'd', 'mixed', 'c', 'd', 'latents')
LEFT_FIRST = True
CORE_PIECES = 2
CLIP_PIECES = {"a": 1, "b": 1, "c": 1, "d": 1}
LIMITS = {"share": 1, "query_back": 1, "key_back": 1, "weight_total": 1}
LANES = 128
BF = jnp.bfloat16
F32 = jnp.float32
ANY = pl.BlockSpec(memory_space=pl.ANY)
HBM = pl.BlockSpec(memory_space=pltpu.HBM)
VMEM = pl.BlockSpec(memory_space=pltpu.VMEM)
OVER_LAST = (((1,), (1,)), ((), ()))
OVER_FIRST = (((0,), (0,)), ((), ()))


def swap(value, axis, distance):
    count = lax.axis_size(axis)
    return lax.ppermute(value, axis, [(i, i ^ distance) for i in range(count)])


def unxor(pieces, place):
    pieces = list(pieces)
    for bit in range((len(pieces) - 1).bit_length()):
        odd = ((place >> bit) & 1) == 1
        pieces = [jnp.where(odd, pieces[j ^ (1 << bit)], pieces[j]) for j in range(len(pieces))]
    return pieces


def inv_rms(values):
    return lax.rsqrt(jnp.mean(values * values, axis=-1, keepdims=True) + EPSILON)


def norm_back(raw, gains, upstream):
    inv_norm = inv_rms(raw)
    inner_dot = jnp.mean(upstream * gains * raw, axis=-1, keepdims=True)
    return inv_norm * (gains * upstream - raw * inv_norm * inv_norm * inner_dot)


def round_up(value, step):
    return -(-value // step) * step


def head_place(heads):
    sharers = lax.axis_size("seq") // heads
    seq = lax.axis_index("seq")
    return seq // sharers, seq % sharers


def call(kernel, name, out, args, scratch, mib, flops, after=(), specs=None, copies=0):
    mib = LIMITS.get(name, mib)
    given, late = len(args), len(after)

    def body(*refs):
        kernel(*refs[:given], *refs[given + late :])

    scratch = [pltpu.VMEM(*s) for s in scratch]
    if copies:
        scratch.append(pltpu.SemaphoreType.DMA((copies,)))
    return list(
        pl.pallas_call(
            body,
            out_shape=[jax.ShapeDtypeStruct(*o) for o in out],
            in_specs=(specs or [VMEM] * given) + [ANY] * late,
            out_specs=[VMEM] * len(out),
            scratch_shapes=scratch,
            compiler_params=pltpu.CompilerParams(vmem_limit_bytes=int(mib * (1 << 20))),
            cost_estimate=pl.CostEstimate(
                flops=0, bytes_accessed=COST.get(name, 1) << 10, transcendentals=0
            ),
            name=name,
        )(*args, *after)
    )


class Copies:
    def __init__(self, sems):
        self.sems, self.made = sems, []

    def start(self, source, target):
        copy = pltpu.make_async_copy(source, target, self.sems.at[len(self.made)])
        copy.start()
        self.made.append(copy)

    def wait(self):
        for copy in self.made:
            copy.wait()


def stage_kernel(count, *refs):
    copies = Copies(refs[-1])
    for source, target in zip(refs[:count], refs[count : 2 * count]):
        copies.start(source, target)
    copies.wait()


def columns_of(place, width):
    return pl.ds(pl.multiple_of(place * width, LANES), width)


def spread(pieces, target):
    place = lax.axis_index("mp")
    width = pieces[0].shape[-1]
    for t, piece in enumerate(pieces):
        if len(pieces) == 1:
            target[...] = piece[...]
        else:
            target[:, columns_of(place ^ t, width)] = piece[...]


def width_pieces(value):
    pieces = [value] + [swap(value, "mp", t) for t in range(1, lax.axis_size("mp"))]
    if value.shape[-1] % LANES:
        return [jnp.concatenate(unxor(pieces, lax.axis_index("mp")), axis=-1)]
    return pieces


def width_outs(rows, width, width_part, extra=0):
    if width_part % LANES:
        return [((rows, width), F32)]
    others = width // width_part - 1
    return [((rows, width_part), F32)] + [((rows, width_part + extra), BF)] * others


def write_width(source, refs):
    if len(refs) == 1:
        refs[0][...] = source[...]
        return
    place = lax.axis_index("mp")
    width = refs[0].shape[-1]
    for t, ref in enumerate(refs):
        ref[:, :width] = source[:, columns_of(place ^ t, width)].astype(ref.dtype)


def width_sum(parts, width_part):
    place = lax.axis_index("mp")
    count = lax.axis_size("mp")
    if width_part % LANES:
        whole = parts[0]
        parts = [
            lax.dynamic_slice_in_dim(whole, (place ^ t) * width_part, width_part, 1)
            for t in range(count)
        ]
    total, beside = parts[0], []
    for t in range(1, count):
        got = swap(parts[t].astype(BF), "mp", t)
        total = total + got[:, :width_part].astype(F32)
        beside.append(got[:, width_part : width_part + 3])
    return total, beside


def project_kernel(heads, width_count, *refs):
    q_gain_ref, k_gain_ref, weight_ref, mod_ref = refs[:4]
    inputs = refs[4 : 4 + width_count]
    refs = refs[4 + width_count :]
    pieces = refs[:heads]
    hidden_ref, raw_ref, inv_ref, inputs_s, values_s = refs[heads:]
    spread(inputs, inputs_s)
    model_width = inputs_s.shape[1]
    values = inputs_s[...].astype(F32)
    inv_norm = inv_rms(values)
    inv_ref[...] = inv_norm
    scale = 1.0 + mod_ref[:, :model_width].astype(F32)
    hidden = (values * inv_norm * scale).astype(BF)
    hidden_ref[...] = hidden
    for at in range(2):
        raw_ref[at] = jnp.dot(hidden, weight_ref[at], preferred_element_type=F32)
    values_s[...] = jnp.dot(hidden, weight_ref[2], preferred_element_type=F32).astype(BF)
    dim = values_s.shape[1] // heads
    head, _ = head_place(heads)
    for t in range(heads):
        own = head ^ t
        columns = columns_of(own, dim)
        for at, gain_ref in enumerate((q_gain_ref, k_gain_ref)):
            raw = raw_ref[at, :, columns]
            pieces[t][at] = (raw * inv_rms(raw) * gain_ref[pl.ds(own, 1), :]).astype(BF)
        pieces[t][2] = values_s[:, columns]


def upstream_kernel(heads, width_count, *refs):
    weight_ref, mod_ref = refs[:2]
    upstream = refs[2 : 2 + width_count]
    refs = refs[2 + width_count :]
    pieces = refs[:heads]
    grad_ref, upstream_s, heads_s = refs[heads:]
    spread(upstream, upstream_s)
    model_width = upstream_s.shape[1]
    grad = (upstream_s[...].astype(F32) * mod_ref[:, model_width:].astype(F32)).astype(BF)
    grad_ref[...] = grad
    heads_s[...] = lax.dot_general(
        grad, weight_ref[...], OVER_LAST, preferred_element_type=F32
    ).astype(BF)
    dim = heads_s.shape[1] // heads
    head, _ = head_place(heads)
    for t in range(heads):
        pieces[t][...] = heads_s[:, columns_of(head ^ t, dim)]


def turn_kernel(count, clips, source_ref, *refs):
    pieces, turned_s = refs[:clips], refs[clips]
    span, rows = turned_s.shape[-2], source_ref.shape[0]
    clip = lax.axis_index("dp")
    turned_s[...] = jnp.zeros_like(turned_s)
    turned = jnp.transpose(source_ref[...].astype(F32))
    for b in range(count * clips):
        turned_s[b % clips, b // clips, :, :rows] = turned[b * span : (b + 1) * span].astype(BF)
    for w in range(clips):
        pieces[w][...] = turned_s[clip ^ w]


def turned(source, after):
    count, clips = lax.axis_size("seq"), lax.axis_size("dp")
    rows, width = source.shape
    shape = (count, width // (count * clips), round_up(rows, LANES))
    pieces = call(
        functools.partial(turn_kernel, count, clips),
        "turn",
        [(shape, BF)] * clips,
        [source],
        [((clips,) + shape, BF)],
        6,
        1 << 27,
        after,
    )
    return [pieces[0]] + [swap(pieces[w], "dp", w) for w in range(1, clips)]


def gather_kernel(heads, *refs):
    out_ref = refs[heads]
    for t in range(heads):
        out_ref[t] = refs[t][1:]


def attention_kernel(heads, sharers, rows, block, factor, *refs):
    key_group_ref, query_group_ref = refs[:2]
    at = 2
    own = refs[at : at + heads]
    at += heads
    shared = refs[at : at + sharers - 1]
    at += sharers - 1
    ups = refs[at : at + heads]
    at += heads
    outs = refs[at : at + heads]
    at += heads
    key_grads = refs[at : at + sharers]
    at += sharers
    key_s, value_s, query_s, up_s, out_s, dk_s, dv_s, sems = refs[at:]
    head, part = head_place(heads)
    dim = key_s.shape[-1]
    span = heads * sharers * rows
    total = heads * rows
    copies = Copies(sems)
    for t in range(heads):
        m = head ^ t
        for u in range(1, sharers):
            piece = shared[u - 1].at[t]
            copies.start(piece.at[0], key_s.at[m * sharers + (part ^ u)])
            copies.start(piece.at[1], value_s.at[m * sharers + (part ^ u)])
        if t:
            copies.start(own[t].at[0], query_s.at[m])
            copies.start(own[t].at[1], key_s.at[m * sharers + part])
            copies.start(own[t].at[2], value_s.at[m * sharers + part])
            copies.start(ups[t], up_s.at[m])
    query_s[head] = own[0][0]
    key_s[head * sharers + part] = own[0][1]
    value_s[head * sharers + part] = own[0][2]
    up_s[head] = ups[0][...]
    dk_s[...] = jnp.zeros_like(dk_s)
    dv_s[...] = jnp.zeros_like(dv_s)
    group_col = jnp.transpose(jnp.broadcast_to(key_group_ref[...], (128, span)))
    group_col = jnp.concatenate([group_col] * (-(-block // 128)), axis=1)[:, :block]
    copies.wait()
    keys = key_s[...].reshape(span, dim)
    values = value_s[...].reshape(span, dim)
    queries = query_s[...].reshape(total, dim)
    upstream = up_s[...].reshape(total, dim)
    scale = factor * math.log2(math.e)
    for j in range(total // block):
        last = ((j + 1) * block - 1) // rows
        reach = min(span, round_up((last + 1) * sharers * rows + GROUP_MOST - 1, 128))
        lanes = slice(j * block, (j + 1) * block)
        query = queries[lanes]
        up = upstream[lanes]
        key = keys[:reach]
        value = values[:reach]
        logits = lax.dot_general(key, query, OVER_LAST, preferred_element_type=F32)
        logits = jnp.where(group_col[:reach] <= query_group_ref[:, lanes], logits, NEG_FILL)
        row_max = jnp.max(logits, axis=0, keepdims=True)
        unnorm = jnp.exp2((logits - row_max) * scale)
        inverse = 1.0 / jnp.sum(unnorm, axis=0, keepdims=True)
        out = lax.dot_general(value, unnorm.astype(BF), OVER_FIRST, preferred_element_type=F32)
        out = (out * inverse).astype(BF)
        up_t = jnp.transpose(up.astype(F32))
        out_dot = jnp.sum(up_t * out.astype(F32), axis=0, keepdims=True)
        probs = unnorm * inverse
        grad_probs = lax.dot_general(value, up, OVER_LAST, preferred_element_type=F32)
        grad_logits = (probs * (grad_probs - out_dot)).astype(BF)
        grad_query = lax.dot_general(key, grad_logits, OVER_FIRST, preferred_element_type=F32)
        out_s[0, lanes, :] = jnp.transpose(out.astype(F32)).astype(BF)
        out_s[1, lanes, :] = jnp.transpose(grad_query * factor).astype(BF)
        dk_s[:reach, :] += jnp.dot(grad_logits, query, preferred_element_type=F32)
        dv_s[:reach, :] += jnp.dot(probs.astype(BF), up, preferred_element_type=F32)
    for t in range(heads):
        m = head ^ t
        for u in range(sharers):
            there = pl.ds(pl.multiple_of((m * sharers + (part ^ u)) * rows, 64), rows)
            ref = key_grads[u]
            ref[t, 0] = (dk_s[there, :] * factor).astype(ref.dtype)
            ref[t, 1] = dv_s[there, :].astype(ref.dtype)
        here = pl.ds(pl.multiple_of(m * rows, 64), rows)
        outs[t][...] = out_s[:, here, :]


def attention_groups(part, group_ids, clip_length, heads, sharers):
    span = group_ids.shape[0]
    positions = lax.iota(jnp.int32, span)
    key_group = jnp.where(positions < clip_length, group_ids, NO_GROUP)[None, :]
    query_group = lax.dynamic_index_in_dim(
        group_ids.reshape(heads, sharers, span // (heads * sharers)), part, 1, keepdims=False
    ).reshape(1, span // sharers)
    return key_group, query_group


def attention(key_group, query_group, own, shared, ups, after):
    heads = len(own)
    sharers = len(shared) + 1
    rows, width = ups[0].shape
    span = heads * sharers * rows
    total = heads * rows
    block = 256 if total % 256 == 0 else total
    pair = (2, rows, width)
    got = call(
        functools.partial(attention_kernel, heads, sharers, rows, block, width ** (-0.5)),
        "attention",
        [(pair, BF)] * heads + [((heads,) + pair, F32)] + [((heads,) + pair, BF)] * (sharers - 1),
        [key_group, query_group, *own, *shared, *ups],
        [
            ((heads * sharers, rows, width), BF),
            ((heads * sharers, rows, width), BF),
            ((heads, rows, width), BF),
            ((heads, rows, width), BF),
            ((2, total, width), BF),
            ((span, width), F32),
            ((span, width), F32),
        ],
        ATTENTION_MIB,
        12 * total * span * width,
        after,
        [VMEM] * 3
        + [HBM] * (heads - 1 + sharers - 1)
        + [VMEM]
        + [HBM] * (heads - 1),
        2 * heads * (sharers - 1) + 4 * (heads - 1),
    )
    return got[:heads], got[heads:]


def share_kernel(sharers, *refs):
    terms, sums = refs[:sharers], refs[sharers:]
    for t, ref in enumerate(sums):
        total = terms[0][t]
        for u in range(1, sharers):
            total = total + terms[u][t].astype(F32)
        ref[...] = total.astype(BF)


def query_kernel(heads, parts, *refs):
    gain_ref, raw_ref = refs[:2]
    pieces, outs = refs[2 : 2 + heads], refs[2 + heads :]
    row_refs, grad_refs = outs[:parts], outs[parts:]
    inner = raw_ref.shape[-1]
    dim = inner // heads
    head, _ = head_place(heads)
    for t in range(heads):
        own = head ^ t
        write_pieces(row_refs, own, pieces[t][0])
        grad = norm_back(
            raw_ref[0, :, columns_of(own, dim)],
            gain_ref[pl.ds(own, 1), :],
            pieces[t][1].astype(F32),
        )
        write_pieces(grad_refs, own, grad.astype(BF))


def key_kernel(heads, parts, *refs):
    gain_ref, raw_ref = refs[:2]
    pieces, outs = refs[2 : 2 + heads], refs[2 + heads :]
    key_refs, value_refs = outs[:parts], outs[parts:]
    inner = raw_ref.shape[-1]
    dim = inner // heads
    head, _ = head_place(heads)
    for t in range(heads):
        own = head ^ t
        grad = norm_back(
            raw_ref[1, :, columns_of(own, dim)],
            gain_ref[pl.ds(own, 1), :],
            pieces[t][0].astype(F32),
        )
        write_pieces(key_refs, own, grad.astype(BF))
        write_pieces(value_refs, own, pieces[t][1])


def join_columns(refs):
    return jnp.concatenate([ref[...] for ref in refs], axis=1)


def mix_kernel(parts, *refs):
    rows, weight_ref, whole_s = refs[:parts], refs[parts], refs[-1]
    whole_s[...] = jnp.dot(join_columns(rows), weight_ref[...], preferred_element_type=F32)
    write_width(whole_s, refs[parts + 1 : -1])


def hidden_kernel(width_count, parts, *refs):
    grads = []
    for part in parts:
        grads.append(join_columns(refs[:part]))
        refs = refs[part:]
    refs = (None,) * 3 + refs
    weight_ref, mod_ref, inv_ref = refs[3:6]
    inputs = refs[6 : 6 + width_count]
    dot_ref = refs[6 + width_count]
    outs = refs[7 + width_count : -4]
    whole_s, inputs_s, weight_s, sems = refs[-4:]
    copies = Copies(sems)
    for at in range(3):
        copies.start(weight_ref.at[at], weight_s.at[at])
    spread(inputs, inputs_s)
    total = 0.0
    for at, grad in enumerate(grads):
        copies.made[at].wait()
        total = total + lax.dot_general(
            grad, weight_s[at], OVER_LAST, preferred_element_type=F32
        )
    whole_s[...] = total
    write_width(whole_s, outs)
    model_width = inputs_s.shape[1]
    scale = 1.0 + mod_ref[:, :model_width].astype(F32)
    normed = inputs_s[...].astype(F32) * inv_ref[...]
    dot = jnp.sum(whole_s[...] * scale * normed, axis=1, keepdims=True)
    dot_ref[...] = dot
    for ref in outs[1:]:
        high = dot.astype(BF).astype(F32)
        middle = (dot - high).astype(BF).astype(F32)
        low = dot - high - middle
        lane = lax.broadcasted_iota(jnp.int32, (dot.shape[0], LANES), 1)
        beside = jnp.where(lane == 0, high, jnp.where(lane == 1, middle, low))
        ref[:, outs[0].shape[1] :] = beside.astype(BF)


def halve(total, step, sends, keep_ref):
    odd = (lax.axis_index("seq") // step) % 2 == 1
    each = sends[0].shape[0]
    for b in range(total.shape[0] // 2):
        first, second = total[2 * b], total[2 * b + 1]
        keep_ref[b] = jnp.where(odd, second, first)
        sends[b // each][b % each] = jnp.where(odd, first, second).astype(BF)


def outer_kernel(clips, pieces, parts, *refs):
    rights, lefts = refs[: clips * pieces], refs[clips * pieces : clips * pieces + clips]
    sends, (keep_ref, total_s) = refs[-2 - parts : -2], refs[-2:]
    blocks, span, lanes = lefts[0].shape
    rows, width = rights[0].shape
    for at in range(pieces):
        total = 0.0
        for w, left in enumerate(lefts):
            left = left[...].reshape(blocks * span, lanes)[:, :rows]
            right = rights[w * pieces + at][...]
            total = total + jnp.dot(left, right, preferred_element_type=F32)
        total_s[:, :, at * width : (at + 1) * width] = total.reshape(blocks, span, width)
    halve(total_s, 1, sends, keep_ref)


def step_kernel(step, parts, *refs):
    gots, (kept_ref, send_ref, keep_ref) = refs[:parts], refs[parts:]
    got = jnp.concatenate([ref[...].astype(F32) for ref in gots], axis=0)
    halve(kept_ref[...] + got, step, [send_ref], keep_ref)


def halves(blocks, span, width, parts=1):
    send = (blocks // 2 // parts, span, width)
    return [(send, BF)] * parts + [((blocks // 2, span, width), F32)]


def clip_pieces(name, width):
    return CLIP_PIECES[name] if width % (CLIP_PIECES[name] * LANES) == 0 else 1


def write_pieces(pieces, place, value):
    width, dim = pieces[0].shape[1], value.shape[1]
    each = width // dim
    for at, piece in enumerate(pieces):
        if len(pieces) == 1:
            piece[:, columns_of(place, dim)] = value
        else:

            @pl.when(place // each == at)
            def _(piece=piece):
                piece[:, columns_of(place % each, dim)] = value


class WeightSum:
    def __init__(self, name, lefts, rights):
        self.name, self.pieces = name, len(rights)
        self.rights = list(rights)
        for w in range(1, lax.axis_size("dp")):
            self.rights.extend(swap(right, "dp", w) for right in rights)
        self.lefts, self.step = lefts, 1

    def outer(self, after):
        blocks, span, _ = self.lefts[0].shape
        rows, width = self.rights[0].shape
        width = width * self.pieces
        parts = min(CORE_PIECES, blocks // 2)
        *self.sends, self.keep = call(
            functools.partial(outer_kernel, len(self.lefts), self.pieces, parts),
            "weight_sum_" + self.name,
            halves(blocks, span, width, parts),
            [*self.rights, *self.lefts],
            [((blocks, span, width), F32)],
            12,
            2 * blocks * span * rows * width * len(self.rights),
            after,
        )
        return [self.sends[0]]

    def exchange(self):
        self.gots = [swap(send, "seq", self.step) for send in self.sends]
        self.step *= 2

    def halve(self, after):
        *self.sends, self.keep = call(
            functools.partial(step_kernel, self.step, len(self.gots)),
            "weight_step_%s%d" % (self.name, self.step),
            halves(*self.keep.shape),
            [*self.gots, self.keep],
            [],
            4,
            1 << 22,
            after,
        )
        return [self.sends[0]]


def total_kernel(*refs):
    in_ref, out_ref = refs[-2:]
    inner = out_ref.shape[1]
    targets = [out_ref, in_ref.at[0], in_ref.at[1], in_ref.at[2]]
    for got, kept in zip(refs[0:-2:2], refs[1:-2:2]):
        for at in range(got.shape[2] // inner):
            columns = slice(at * inner, (at + 1) * inner)
            targets.pop(0)[...] = got[0, :, columns].astype(F32) + kept[0, :, columns]


def finish_mix_kernel(latents_ref, mod_ref, own_ref, *refs):
    gots, out_ref = refs[:-1], refs[-1]
    width = own_ref.shape[1]
    place = lax.axis_index("mp") + mod_ref.shape[1] // 2 // width
    gate = mod_ref[:, columns_of(place, width)].astype(F32)
    total = own_ref[...]
    for got in gots:
        total = total + got[...].astype(F32)
    out_ref[...] = (latents_ref[...].astype(F32) + gate * total).astype(BF)


def finish_latents_kernel(latents_ref, upstream_ref, mod_ref, inv_ref, dot_ref, own_ref, *refs):
    gots, out_ref = refs[:-1], refs[-1]
    width = own_ref.shape[1]
    scale = 1.0 + mod_ref[:, columns_of(lax.axis_index("mp"), width)].astype(F32)
    total, dot = own_ref[...], dot_ref[...]
    for got in gots:
        total = total + got[:, :width].astype(F32)
        lane = lax.broadcasted_iota(jnp.int32, (got.shape[0], LANES), 1)
        beside = jnp.where(lane < 3, got[:, width:].astype(F32), 0.0)
        dot = dot + jnp.sum(beside, axis=1, keepdims=True)
    inv_norm = inv_ref[...]
    normed = latents_ref[...].astype(F32) * inv_norm
    mean = dot * (1.0 / (mod_ref.shape[1] // 2))
    grad = inv_norm * (total * scale - normed * mean)
    out_ref[...] = (upstream_ref[...].astype(F32) + grad).astype(BF)


def finish_mix(latents, mod, parts, after):
    width = latents.shape[1]
    if width % LANES:
        place = lax.axis_index("mp") * width + mod.shape[1] // 2
        gate = lax.dynamic_slice_in_dim(mod, place, width, 1).astype(F32)
        total, _ = width_sum(parts, width)
        return (latents.astype(F32) + gate * total).astype(BF), after
    gots = [swap(parts[t], "mp", t) for t in range(1, len(parts))]
    (mixed,) = call(
        finish_mix_kernel,
        "finish_mix",
        [(latents.shape, BF)],
        [latents, mod, parts[0], *gots],
        [],
        4,
        1 << 22,
        after,
    )
    return mixed, [mixed]


def finish_latents(latents, grad_out, mod, inv_norm, dot, parts, after):
    width = latents.shape[1]
    if width % LANES:
        total, _ = width_sum(parts, width)
        dot = sum([swap(dot, "mp", t) for t in range(1, lax.axis_size("mp"))], dot)
        place = lax.axis_index("mp") * width
        scale = 1.0 + lax.dynamic_slice_in_dim(mod, place, width, 1).astype(F32)
        normed = latents.astype(F32) * inv_norm
        grad = inv_norm * (total * scale - normed * (dot / (mod.shape[1] // 2)))
        return (grad_out.astype(F32) + grad).astype(BF), after
    gots = [swap(parts[t], "mp", t) for t in range(1, len(parts))]
    (grad,) = call(
        finish_latents_kernel,
        "finish_latents",
        [(latents.shape, BF)],
        [latents, grad_out, mod, inv_norm, dot, parts[0], *gots],
        [],
        4,
        1 << 22,
        after,
    )
    return grad, [grad]


def on_device(
    latents, grad_out, sync_mod, w_qkv, w_out, q_gain, k_gain, frame_of, group_id, clip_len
):
    latents, grad_out, sync_mod = latents[0], grad_out[0], sync_mod[0]
    frame_of, group_id, clip_len = frame_of[0], group_id[0], clip_len[0]
    rows, width_part = latents.shape
    frame_count = sync_mod.shape[0]
    model_width = sync_mod.shape[1] // 2
    heads, head_dim = q_gain.shape
    inner = heads * head_dim
    count, clips = lax.axis_size("seq"), lax.axis_size("dp")
    sharers = count // heads
    seq = lax.axis_index("seq")
    _, part = head_place(heads)

    inputs = width_pieces(latents)
    width_count = len(inputs)

    back = max(frame_count * j - (FRAME_UP * rows * j) // FRAME_DOWN for j in range(count))
    back = min(frame_count, round_up(max(back, 1), 16))
    earlier = lax.ppermute(
        sync_mod[frame_count - back :], "seq", [(i, i + 1) for i in range(count - 1)]
    )
    window = jnp.concatenate([earlier, sync_mod], axis=0)
    local_frame = frame_of - (seq * frame_count - back)
    selector = (
        local_frame[:, None] == lax.iota(jnp.int32, frame_count + back)[None, :]
    ).astype(BF)
    mod = jnp.dot(selector, window, preferred_element_type=F32).astype(BF)

    key_group, query_group = attention_groups(part, group_id, clip_len, heads, sharers)
    weight = jnp.transpose(w_qkv, (1, 0, 2))
    weight_far = weight
    staged = [weight, w_out, key_group, query_group, grad_out]
    weight, w_out, key_group, query_group, grad_out = call(
        functools.partial(stage_kernel, len(staged)),
        "stage",
        [(array.shape, array.dtype) for array in staged],
        staged,
        [],
        2,
        1 << 22,
        [mod],
        [HBM, HBM, VMEM, VMEM, HBM],
        len(staged),
    )
    upstream = width_pieces(grad_out)
    got = call(
        functools.partial(project_kernel, heads, width_count),
        "project",
        [((3, rows, head_dim), BF)] * heads
        + [((rows, model_width), BF), ((2, rows, inner), F32), ((rows, 1), F32)],
        [q_gain, k_gain, weight, mod, *inputs],
        [((rows, model_width), BF), ((rows, inner), BF)],
        8,
        6 * rows * model_width * inner,
    )
    own, (hidden, raw, inv_norm) = got[:heads], got[heads:]
    own = [own[0]] + [swap(own[t], "seq", t * sharers) for t in range(1, heads)]
    left_hidden = turned(hidden, [])
    got = call(
        functools.partial(upstream_kernel, heads, width_count),
        "upstream",
        [((rows, head_dim), BF)] * heads + [((rows, model_width), BF)],
        [w_out, mod, *upstream],
        [((rows, model_width), BF), ((rows, inner), BF)],
        8,
        2 * rows * model_width * inner,
        left_hidden[:1],
    )
    ups, grad_attn = got[:heads], got[heads]
    left_grad = turned(grad_attn, [])
    ups = [ups[0]] + [swap(ups[t], "seq", t * sharers) for t in range(1, heads)]
    (keys_values,) = call(
        functools.partial(gather_kernel, heads),
        "gather",
        [((heads, 2, rows, head_dim), BF)],
        own,
        [],
        2,
        0,
        ups[1:],
    )
    shared = [swap(keys_values, "seq", u) for u in range(1, sharers)]


    outs, key_grads = attention(key_group, query_group, own, shared, ups, [*left_hidden[1:], left_grad[0]])
    terms = key_grads[:1] + [swap(key_grads[u], "seq", u) for u in range(1, sharers)]
    pair = (2, rows, head_dim)
    back_out = [outs[0]] + [swap(outs[t], "seq", t * sharers) for t in range(1, heads)]
    state = {}

    def cut(names, made):
        first = clip_pieces(names[0], inner)
        return made[:first], made[first:]

    def pair_outs(names):
        outs = []
        for name in names:
            pieces = clip_pieces(name, inner)
            outs.extend([((rows, inner // pieces), BF)] * pieces)
        return outs


    def share(after):
        sums = call(
            functools.partial(share_kernel, sharers),
            "share",
            [(pair, BF)] * heads,
            terms,
            [],
            4,
            1 << 24,
            left_grad[1:] if LEFT_FIRST else (),
        )
        state["back_key"] = sums[:1] + [
            swap(sums[t], "seq", t * sharers) for t in range(1, heads)
        ]
        return sums[:1]

    def query(after):
        made = call(
            functools.partial(query_kernel, heads, clip_pieces("a", inner)),
            "query_back",
            pair_outs("ab"),
            [q_gain, raw, *back_out],
            [],
            4,
            1 << 24,
            after,
        )
        state["rows"], state["query"] = cut("ab", made)
        state["a"] = WeightSum("a", left_grad, state["rows"])
        state["b"] = WeightSum("b", left_hidden, state["query"])
        return made[:1]

    def mix(after):
        state["parts"] = call(
            functools.partial(mix_kernel, len(state["rows"])),
            "mix",
            width_outs(rows, model_width, width_part),
            [*state["rows"], w_out],
            [((rows, model_width), F32)],
            8,
            2 * rows * model_width * inner,
            after,
        )
        return state["parts"][:1]

    def key(after):
        made = call(
            functools.partial(key_kernel, heads, clip_pieces("c", inner)),
            "key_back",
            pair_outs("cd"),
            [k_gain, raw, *state["back_key"]],
            [],
            4,
            1 << 24,
            after,
        )
        state["key"], state["value"] = cut("cd", made)
        state["c"] = WeightSum("c", left_hidden, state["key"])
        state["d"] = WeightSum("d", left_hidden, state["value"])
        return made[:1]

    def advance(name, after):
        total = state[name]
        if hasattr(total, "keep") and total.keep.shape[0] == 1:
            return after
        token = total.halve(after) if hasattr(total, "keep") else total.outer(after)
        total.exchange()
        return token

    def hidden_back(after):
        grads = [state[name] for name in ("query", "key", "value")]
        got = call(
            functools.partial(hidden_kernel, width_count, [len(g) for g in grads]),
            "hidden_back",
            [((rows, 1), F32)] + width_outs(rows, model_width, width_part, LANES),
            [*sum(grads, []), weight_far, mod, inv_norm, *inputs],
            [
                ((rows, model_width), F32),
                ((rows, model_width), BF),
                (weight_far.shape, BF),
            ],
            10,
            6 * rows * model_width * inner,
            after,
            [VMEM] * sum(len(g) for g in grads) + [HBM] + [VMEM] * (2 + width_count),
            3,
        )
        state["dot"], state["hidden"] = got[0], got[1:]
        return [state["dot"]]

    def finish(name, after):
        if name == "mixed":
            state["mixed"], token = finish_mix(latents, mod, state["parts"], after)
        else:
            state["latents"], token = finish_latents(
                latents, grad_out, mod, inv_norm, state["dot"], state["hidden"], after
            )
        return token

    steps = dict(share=share, query=query, mix=mix, key=key, hidden=hidden_back)
    for name in "abcd":
        steps[name] = functools.partial(advance, name)
    for name in ("mixed", "latents"):
        steps[name] = functools.partial(finish, name)
    token = ()
    for name in ORDER:
        token = steps[name](token)
    totals = [state[name] for name in "abcd"]
    while max(total.keep.shape[0] for total in totals) > 1:
        for total in totals:
            if total.keep.shape[0] == max(other.keep.shape[0] for other in totals):
                token = total.halve(token)
                total.exchange()
    span = totals[0].keep.shape[1]
    pieces = []
    for total in totals:
        pieces.extend([total.gots[0], total.keep])
    grad_wqkv, grad_wout = call(
        total_kernel,
        "weight_total",
        [((3, span, inner), F32), ((span, inner), F32)],
        pieces,
        [],
        4,
        1 << 22,
    )
    mixed, grad_latents = state["mixed"], state["latents"]
    return (
        mixed[None],
        grad_latents[None],
        jnp.transpose(grad_wqkv, (1, 0, 2)),
        jnp.transpose(grad_wout),
    )


def solution(mesh):
    in_specs = (
        P("dp", "seq", "mp"),
        P("dp", "seq", "mp"),
        P("dp", "seq", None),
        P(None, None, "mp"),
        P("mp", None),
        P("mp", None),
        P("mp", None),
        P("dp", "seq"),
        P("dp", None),
        P("dp"),
    )
    out_specs = (
        P("dp", "seq", "mp"),
        P("dp", "seq", "mp"),
        P(("seq", "dp"), None, "mp"),
        P("mp", ("seq", "dp")),
    )
    return jax.shard_map(
        on_device, mesh=mesh, in_specs=in_specs, out_specs=out_specs, check_vma=False
    )
```
